512 devices in a mesh: depth: 16 (over x_hi, z), scan: 32 (over x_lo, y, core).
Axes of the slice: x: 4 (x_hi: 2, x_lo: 2; x = x_hi * 2 + x_lo), y: 8, z: 8, core: 2. Of those that a mesh axis runs over, the one named last changes fastest.
Arguments:
- object_slices: float32 [16, 2, 4096, 384], P('depth', None, 'scan'), may hold values from -1.25 to 1.25, as said below
- probe: float32 [2, 256, 256], replicated, may hold values from -4 to 4
- offsets: int32 [64, 2], P('scan'), may hold values from 0 to 128
- intensity: float32 [64, 256, 256], P('scan'), may hold values from 0.03 to 1
Outputs:
- object_grad: float32 [16, 2, 4096, 384], P('depth', None, 'scan')
- probe_grad: float32 [2, 256, 256], P(None, 'scan', 'depth')
The draws below stay inside these ranges and needn't reach their ends.
Inputs may be any that keep to these rules, and one draw needn't show every extreme that they name: `offsets`: column 0 is a window's first row counted from 128 rows above the first object row of its scan index, wrapping around the object; column 1 is its first column. `object_slices`: real and imaginary parts of each slice's transmission.
All inputs are finite; a program needn't handle non-finite values.
Results may differ from the reference program's by a relative error of at most 0.035.
Values may be sent and summed in bfloat16 or wider, within the bound.
A program may use at most 64 MiB of HBM per device.

```python
import math
import jax
import jax.numpy as jnp
from jax import lax

PROBE = 256
TILE = 128
HALO = 128
POS_DEV = 2
SLICES = 16
ROWS = 4096
OBJ_COLS = 384
POSITIONS = 64


def draw_object_slices(key, part):
    key = jax.random.fold_in(key, 11)
    size_lookup_key, phase_key = jax.random.split(key)
    grid_shape = (SLICES, ROWS, OBJ_COLS)
    magnitude = jnp.exp(jax.random.uniform(size_lookup_key, grid_shape, jnp.float32, math.log(0.8), math.log(1.25)))
    phases = jax.random.uniform(phase_key, grid_shape, jnp.float32, -math.pi, math.pi)
    return jnp.stack([magnitude * jnp.cos(phases), magnitude * jnp.sin(phases)], axis=1)


def place_ends(entries, rng, smallest, top_value):
    extent = entries.shape
    index_at = [jax.random.randint(jax.random.fold_in(rng, axis), (), 0, extent[axis]) for axis in range(len(extent))]
    entries = entries.at[tuple(index_at)].set(smallest)
    longest = extent.index(max(extent))
    index_at[longest] = (index_at[longest] + 1) % extent[longest]
    return entries.at[tuple(index_at)].set(top_value)


def levels(rng, shape, shards, smallest, high):
    factor_of, own = 1.0, jax.random.fold_in(rng, 6)
    for position, parts in shards:
        steps = jnp.exp(jax.random.uniform(jax.random.fold_in(own, position), (parts,), jnp.float32, smallest / len(shards), high / len(shards)))
        factor_of = factor_of * jnp.repeat(steps, shape[position] // parts).reshape([-1 if axis == position else 1 for axis in range(len(shape))])
    return factor_of


def normal_values(key, dims, spread, reach, kind=jnp.bfloat16):
    values = spread * jax.random.normal(key, dims, jnp.float32)
    return jnp.clip(values, min=-reach, max=reach).astype(kind)


def setup_inputs(seed: int = 0) -> dict:
    key_of = jax.random.split(jax.random.key(seed), 5)
    return {
        "object_slices": draw_object_slices(jax.random.fold_in(key_of[4], 71), 0),
        "probe": normal_values(key_of[1], (2, PROBE, PROBE), 0.45, 4.0, jnp.float32),
        "offsets": place_ends(jax.random.randint(key_of[2], (POSITIONS, 2), 0, HALO + 1), jax.random.fold_in(key_of[2], 1), 0, HALO).astype(jnp.int32),
        "intensity": jnp.clip(jnp.exp(math.log(1.0) - 3.506558 * jax.random.uniform(key_of[3], (POSITIONS, PROBE, PROBE), jnp.float32) ** levels(key_of[3], (POSITIONS, PROBE, PROBE), ((0, 32),), -0.2, 0.2)), 0.03, 1.0),
    }


PHASE_SCALE = 16.0

def dft_table(length, sign_value):
    places = jnp.arange(length, dtype=jnp.int32)
    product = places[:, None] * places[None, :] % length
    angles = product.astype(jnp.float32) * jnp.float32(2.0 * math.pi / length)
    factor = jnp.float32(1.0 / math.sqrt(length))
    cosine = jnp.cos(angles) * factor
    sine_part = jnp.sin(angles) * factor * sign_value
    top_pair = jnp.stack([cosine, sine_part])
    lower_edge_pair = jnp.stack([-sine_part, cosine])
    return jnp.stack([top_pair, lower_edge_pair])

def kernel_table(length):
    places = jnp.arange(length, dtype=jnp.int32)
    shifted = ((places + length // 2) % length - length // 2).astype(jnp.float32) / jnp.float32(length)
    squares = shifted[:, None] * shifted[:, None] + shifted[None, :] * shifted[None, :]
    phases = jnp.float32(-PHASE_SCALE * math.pi) * squares
    return jnp.stack([jnp.cos(phases), jnp.sin(phases)])

def complex_mul(leading_factor, factor_two):
    real_part = leading_factor[0] * factor_two[0] - leading_factor[1] * factor_two[1]
    imag_part = leading_factor[0] * factor_two[1] + leading_factor[1] * factor_two[0]
    return jnp.stack([real_part, imag_part])

def conj_mul(leading_factor, factor_two):
    real_part = leading_factor[0] * factor_two[0] + leading_factor[1] * factor_two[1]
    imag_part = leading_factor[0] * factor_two[1] - leading_factor[1] * factor_two[0]
    return jnp.stack([real_part, imag_part])

def transform(values, dft_matrix):
    initial_sweep = jnp.einsum('cjk,cdkl->djl', values, dft_matrix, precision=lax.Precision.HIGHEST)
    return jnp.einsum('xogs,xsn->ogn', dft_matrix, initial_sweep, precision=lax.Precision.HIGHEST)

def propagate(values, forward, inverse, kernel):
    spectrum = transform(values, forward)
    return transform(complex_mul(kernel, spectrum), inverse).astype(jnp.bfloat16)

def back_propagate(values, forward, inverse, kernel):
    spectrum = transform(values, forward)
    return transform(conj_mul(kernel, spectrum), inverse).astype(jnp.bfloat16)

def reference(object_slices, probe, offsets, intensity):
    forward = dft_table(PROBE, -1)
    inverse = dft_table(PROBE, 1)
    kernel = kernel_table(PROBE)
    places = jnp.arange(PROBE, dtype=jnp.int32)

    def one_window(window, carry_pair):
        object_total, probe_total = carry_pair
        top_row = window // POS_DEV * TILE - HALO + offsets[window, 0]
        row_ids = ((top_row + places) % ROWS).astype(jnp.int32)
        column_ids = (offsets[window, 1] + places).astype(jnp.int32)
        patches = object_slices[:, :, row_ids[:, None], column_ids[None, :]]

        def forward_slice(wave_now, patch):
            product = complex_mul(wave_now.astype(jnp.float32), patch)
            return (propagate(product, forward, inverse, kernel), wave_now)
        last_wave, waves = lax.scan(forward_slice, probe.astype(jnp.bfloat16), patches[:-1])
        waves = jnp.concatenate([waves, last_wave[None]], axis=0)
        exit_wave = complex_mul(last_wave.astype(jnp.float32), patches[-1])
        far_wave = transform(exit_wave, forward)
        residual = (far_wave[0] * far_wave[0] + far_wave[1] * far_wave[1] - intensity[window]) * far_wave
        start_grad = transform(residual, inverse).astype(jnp.bfloat16)

        def backward_slice(gradient, inputs_pair):
            wave_now, patch = inputs_pair
            grad_float = gradient.astype(jnp.float32)
            slice_grad = conj_mul(wave_now.astype(jnp.float32), grad_float)
            through = conj_mul(patch, grad_float)
            return (back_propagate(through, forward, inverse, kernel), (slice_grad, through))
        unused, outputs_pair = lax.scan(backward_slice, start_grad, (waves, patches), reverse=True)
        slice_grads, throughs = outputs_pair
        object_total = object_total.at[:, :, row_ids[:, None], column_ids[None, :]].add(slice_grads)
        return (object_total, probe_total + throughs[0])
    object_zero = jnp.zeros((SLICES, 2, ROWS, OBJ_COLS), jnp.float32)
    probe_zero = jnp.zeros((2, PROBE, PROBE), jnp.float32)
    object_grad, probe_grad = lax.fori_loop(0, POSITIONS, one_window, (object_zero, probe_zero))
    return (object_grad, probe_grad)
```

```python
import functools
import math

import jax
import jax.numpy as jnp
import ml_dtypes
import numpy as np
from jax import lax
from jax.experimental import pallas as pl
from jax.experimental.pallas import tpu as pltpu
from jax.sharding import PartitionSpec as P

MESH = pl.DeviceIdType.MESH
N = 256
HALF = 128
TILE = 128
COLS = 384
SLICES = 16
PHASE_SCALE = 16.0
BF = jnp.bfloat16
F32 = jnp.float32


def real_form(table):
    return np.block([[table.real, table.imag], [-table.imag, table.real]])


def tables():
    n = np.arange(N)
    dft = np.exp(-2j * math.pi * (np.outer(n, n) % N) / N) / math.sqrt(N)
    q = ((n + HALF) % N - HALF) / N
    circulant = dft.conj() @ np.diag(np.exp(-1j * PHASE_SCALE * math.pi * q * q)) @ dft
    upper, lower = circulant[:HALF, :HALF], circulant[HALF:, :HALF]
    right = [
        real_form((upper + lower) / 2),
        real_form((upper - lower) / 2),
        real_form(dft[:HALF, 0::2]),
        real_form(dft[:HALF, 1::2]),
    ]
    full = np.stack(right + [t.T for t in right]).astype(np.float32)
    high = full.astype(ml_dtypes.bfloat16)
    low = (full - high.astype(np.float32)).astype(ml_dtypes.bfloat16)
    return np.stack([high, low], axis=1)


def dot(a, b):
    return jnp.dot(a, b, preferred_element_type=F32)


def one_hot(shape, hit):
    r = lax.broadcasted_iota(jnp.int32, shape, 0)
    c = lax.broadcasted_iota(jnp.int32, shape, 1)
    return jnp.where(hit(r, c), 1.0, 0.0).astype(BF)


def halves(x, axis):
    if axis == 0:
        return x[:HALF], x[HALF:]
    return x[:, :HALF], x[:, HALF:]


def butterfly(x, axis):
    first, second = halves(x, axis)
    return first + second, first - second


def join(a, b, axis):
    return jnp.concatenate([a, b], axis=axis)


def right_mul(x, tab, k):
    x = x.astype(BF)
    return dot(x, tab[k, 0]) + dot(x, tab[k, 1])


def left_mul(x, tab, k):
    x = x.astype(BF)
    return dot(tab[k, 0], x) + dot(tab[k, 1], x)


def columns_in(re, im, tab, k):
    sr, dr = butterfly(re, 1)
    si, di = butterfly(im, 1)
    a = right_mul(join(sr, si, 1), tab, k)
    b = right_mul(join(dr, di, 1), tab, k + 1)
    ar, ai = halves(a, 1)
    br, bi = halves(b, 1)
    return join(ar, br, 1), join(ai, bi, 1)


def rows_in(re, im, tab, k):
    sr, dr = butterfly(re, 0)
    si, di = butterfly(im, 0)
    a = left_mul(join(sr, si, 0), tab, k)
    b = left_mul(join(dr, di, 0), tab, k + 1)
    ar, ai = halves(a, 0)
    br, bi = halves(b, 0)
    return join(ar, br, 0), join(ai, bi, 0)


def rows_out(re, im, tab, k):
    re0, re1 = halves(re, 0)
    im0, im1 = halves(im, 0)
    a = left_mul(join(re0, im0, 0), tab, k)
    b = left_mul(join(re1, im1, 0), tab, k + 1)
    ar, ai = halves(a, 0)
    br, bi = halves(b, 0)
    return join(ar + br, ar - br, 0), join(ai + bi, ai - bi, 0)


def columns_out(re, im, tab, k):
    re0, re1 = halves(re, 1)
    im0, im1 = halves(im, 1)
    a = right_mul(join(re0, im0, 1), tab, k)
    b = right_mul(join(re1, im1, 1), tab, k + 1)
    ar, ai = halves(a, 1)
    br, bi = halves(b, 1)
    return join(ar + br, ar - br, 1), join(ai + bi, ai - bi, 1)


def propagate(re, im, tab, right, left):
    re, im = columns_in(re, im, tab, right)
    re, im = rows_in(re, im, tab, left)
    re, im = join(*butterfly(re, 0), 0), join(*butterfly(im, 0), 0)
    return join(*butterfly(re, 1), 1), join(*butterfly(im, 1), 1)


def remote(src, dst, send, recv, axis, index):
    return pltpu.make_async_remote_copy(
        src_ref=src,
        dst_ref=dst,
        send_sem=send,
        recv_sem=recv,
        device_id={axis: index},
        device_id_type=MESH,
    )


def kernel(
    off_ref, obj_ref, probe_ref, int_ref, tab_hbm,
    out_ref, part_ref,
    region, patch, held, waves, current, gout, gin, rim, rim_in, tab, meas,
    halo_send, halo_recv, patch_send, patch_recv, grad_send, grad_recv, rim_send, rim_recv, local_sem,
):
    d = lax.axis_index("depth")
    m = lax.axis_index("scan")
    above, below = lax.rem(m + 31, 32), lax.rem(m + 1, 32)
    core = lax.rem(m, 2)
    x_lo = m // 16
    worker = [j * 8 + lax.rem(4 * core + 2 * j + x_lo, 8) for j in range(2)]
    mine = [d == w for w in worker]
    working = jnp.logical_or(mine[0], mine[1])

    tab_copy = pltpu.make_async_copy(tab_hbm, tab, local_sem.at[0])
    meas_copy = [pltpu.make_async_copy(int_ref.at[j], meas, local_sem.at[1]) for j in range(2)]

    @pl.when(working)
    def _():
        tab_copy.start()

    for j in range(2):

        @pl.when(mine[j])
        def _():
            meas_copy[j].start()

    barrier = pltpu.get_barrier_semaphore()
    for t in (above, below):
        pl.semaphore_signal(barrier, inc=1, device_id={"scan": t}, device_id_type=MESH)
    for j in range(2):

        @pl.when(jnp.logical_not(mine[j]))
        def _():
            pl.semaphore_signal(barrier, inc=1, device_id={"depth": worker[j]}, device_id_type=MESH)

    region[1] = obj_ref[0].astype(BF)

    @pl.when(working)
    def _():
        def greet(k, c):
            @pl.when(jnp.logical_and(k != worker[0], k != worker[1]))
            def _():
                pl.semaphore_signal(barrier, inc=1, device_id={"depth": k}, device_id_type=MESH)

            return c

        lax.fori_loop(0, SLICES, greet, 0)
        pl.semaphore_wait(barrier, 17)

    @pl.when(jnp.logical_not(working))
    def _():
        pl.semaphore_wait(barrier, 4)

    down = remote(region.at[1], region.at[0], halo_send.at[0], halo_recv.at[0], "scan", below)
    up = remote(region.at[1], region.at[2], halo_send.at[1], halo_recv.at[1], "scan", above)
    down.start()
    up.start()
    row_off = [off_ref[j, 0] for j in range(2)]
    col_off = [off_ref[j, 1] for j in range(2)]
    pick_cols = join(
        *[one_hot((COLS, N), lambda r, c, j=j: r == c + col_off[j]) for j in range(2)], 1
    )
    pick_rows = [one_hot((N, 3 * TILE), lambda r, c, j=j: c == r + row_off[j]) for j in range(2)]
    down.wait_recv()
    up.wait_recv()
    for c in range(2):
        strip = jnp.concatenate([region[t, c] for t in range(3)], axis=0)
        narrow = dot(strip, pick_cols).astype(BF)
        for j in range(2):
            patch[j, c] = dot(pick_rows[j], narrow[:, j * N : (j + 1) * N]).astype(BF)

    def patch_copy(j):
        return remote(patch.at[j], held.at[d], patch_send.at[j], patch_recv.at[d], "depth", worker[j])

    def patch_keep(j):
        return pltpu.make_async_copy(patch.at[j], held.at[d], patch_recv.at[d])

    for j in range(2):

        @pl.when(mine[j])
        def _():
            patch_keep(j).start()

        @pl.when(jnp.logical_not(mine[j]))
        def _():
            patch_copy(j).start()

    down.wait_send()
    up.wait_send()

    def work(j):
        tab_copy.wait()
        meas_copy[j].wait()
        even_odd = one_hot(
            (N, N),
            lambda r, c: c == jnp.where(r < HALF, 2 * r, 2 * r - (N - 1)),
        )
        even_odd_t = one_hot(
            (N, N),
            lambda r, c: r == jnp.where(c < HALF, 2 * c, 2 * c - (N - 1)),
        )
        measured = meas[...]
        high = measured.astype(BF)
        low = (measured - high.astype(F32)).astype(BF)
        meas[...] = dot(dot(even_odd, high).astype(BF), even_odd_t) + dot(
            dot(even_odd, low).astype(BF), even_odd_t
        )
        for c in range(2):
            current[c] = probe_ref[c].astype(BF).astype(F32)

        def wait_patch(s):
            @pl.when(s == d)
            def _():
                patch_keep(j).wait()

            @pl.when(s != d)
            def _():
                remote(
                    patch.at[j], held.at[s], patch_send.at[j], patch_recv.at[s], "depth", worker[j]
                ).wait_recv()

        def exit_wave(s):
            wait_patch(s)
            wr, wi = current[0], current[1]
            waves[s, 0] = wr.astype(BF)
            waves[s, 1] = wi.astype(BF)
            pr, pi = held[s, 0].astype(F32), held[s, 1].astype(F32)
            return wr * pr - wi * pi, wr * pi + wi * pr

        def forward(s, carry):
            re, im = exit_wave(s)
            re, im = propagate(re, im, tab, 0, 4)
            current[0] = re
            current[1] = im
            return carry

        lax.fori_loop(0, SLICES - 1, forward, 0)
        re, im = exit_wave(SLICES - 1)
        re, im = columns_in(re, im, tab, 2)
        re, im = rows_in(re, im, tab, 6)
        misfit = re * re + im * im - meas[...]
        re, im = rows_out(misfit * re, misfit * im, tab, 2)
        re, im = columns_out(re, im, tab, 6)
        current[0] = re
        current[1] = im

        def grad_copy(s):
            return remote(gout.at[s], gin.at[j], grad_send.at[s], grad_recv.at[j], "depth", s)

        def grad_keep(s):
            return pltpu.make_async_copy(gout.at[s], gin.at[j], grad_recv.at[j])

        def through(s):
            gr, gi = current[0], current[1]
            wr, wi = waves[s, 0].astype(F32), waves[s, 1].astype(F32)
            gout[s, 0] = (wr * gr + wi * gi).astype(BF)
            gout[s, 1] = (wr * gi - wi * gr).astype(BF)

            @pl.when(s == d)
            def _():
                grad_keep(s).start()

            @pl.when(s != d)
            def _():
                grad_copy(s).start()

            pr, pi = held[s, 0].astype(F32), held[s, 1].astype(F32)
            return pr * gr + pi * gi, pr * gi - pi * gr

        def backward(i, carry):
            re, im = through(SLICES - 1 - i)
            re, im = propagate(re, im, tab, 4, 0)
            current[0] = re
            current[1] = im
            return carry

        lax.fori_loop(0, SLICES - 1, backward, 0)
        re, im = through(0)
        part_ref[0] = re
        part_ref[1] = im

        def sent(s, carry):
            @pl.when(s != d)
            def _():
                grad_copy(s).wait_send()

            return carry

        lax.fori_loop(0, SLICES, sent, 0)

    for j in range(2):

        @pl.when(mine[j])
        def _():
            work(j)

    @pl.when(jnp.logical_not(working))
    def _():
        part_ref[...] = jnp.zeros_like(part_ref)

    for j in range(2):

        @pl.when(jnp.logical_not(mine[j]))
        def _():
            patch_copy(j).wait_send()
            remote(gout.at[0], gin.at[j], grad_send.at[0], grad_recv.at[j], "depth", d).wait_recv()

        @pl.when(mine[j])
        def _():
            pltpu.make_async_copy(gout.at[d], gin.at[j], grad_recv.at[j]).wait()

    put_cols = [one_hot((N, COLS), lambda r, c, j=j: c == r + col_off[j]) for j in range(2)]
    put_rows = join(
        *[one_hot((3 * TILE, N), lambda r, c, j=j: r == c + row_off[j]) for j in range(2)], 1
    )
    for c in range(2):
        wide = join(*[dot(gin[j, c], put_cols[j]).astype(BF) for j in range(2)], 0)
        total = dot(put_rows, wide)
        rim[0, c] = total[:TILE].astype(BF)
        rim[1, c] = total[2 * TILE :].astype(BF)
        out_ref[0, c] = total[TILE : 2 * TILE]
    to_above = remote(rim.at[0], rim_in.at[0], rim_send.at[0], rim_recv.at[0], "scan", above)
    to_below = remote(rim.at[1], rim_in.at[1], rim_send.at[1], rim_recv.at[1], "scan", below)
    to_above.start()
    to_below.start()
    to_above.wait_recv()
    to_below.wait_recv()
    out_ref[0] = out_ref[0] + rim_in[0].astype(F32) + rim_in[1].astype(F32)
    to_above.wait_send()
    to_below.wait_send()


def per_device(tab, object_slices, probe, offsets, intensity):
    vmem = pl.BlockSpec(memory_space=pltpu.VMEM)
    plane = (2, N, N)
    object_grad, part = pl.pallas_call(
        kernel,
        out_shape=(
            jax.ShapeDtypeStruct(object_slices.shape, F32),
            jax.ShapeDtypeStruct(plane, F32),
        ),
        in_specs=[
            pl.BlockSpec(memory_space=pltpu.SMEM),
            vmem,
            vmem,
            pl.BlockSpec(memory_space=pl.ANY),
            pl.BlockSpec(memory_space=pl.ANY),
        ],
        out_specs=(vmem, vmem),
        scratch_shapes=[
            pltpu.VMEM((3, 2, TILE, COLS), BF),
            pltpu.VMEM((2, *plane), BF),
            pltpu.VMEM((SLICES, *plane), BF),
            pltpu.VMEM((SLICES, *plane), BF),
            pltpu.VMEM(plane, F32),
            pltpu.VMEM((SLICES, *plane), BF),
            pltpu.VMEM((2, *plane), BF),
            pltpu.VMEM((2, 2, TILE, COLS), BF),
            pltpu.VMEM((2, 2, TILE, COLS), BF),
            pltpu.VMEM((8, 2, N, N), BF),
            pltpu.VMEM((N, N), F32),
            pltpu.SemaphoreType.DMA((2,)),
            pltpu.SemaphoreType.DMA((2,)),
            pltpu.SemaphoreType.DMA((2,)),
            pltpu.SemaphoreType.DMA((SLICES,)),
            pltpu.SemaphoreType.DMA((SLICES,)),
            pltpu.SemaphoreType.DMA((2,)),
            pltpu.SemaphoreType.DMA((2,)),
            pltpu.SemaphoreType.DMA((2,)),
            pltpu.SemaphoreType.DMA((2,)),
        ],
        compiler_params=pltpu.CompilerParams(
            collective_id=0, has_side_effects=True, vmem_limit_bytes=48 << 20
        ),
        name="ptychography_chains",
    )(offsets, object_slices, probe, intensity, tab)
    partial_sum = lax.psum_scatter(part.astype(BF), "depth", scatter_dimension=2, tiled=True)
    probe_grad = lax.psum_scatter(partial_sum, "scan", scatter_dimension=1, tiled=True)
    return object_grad, probe_grad.astype(F32)


def solution(mesh):
    tab = tables()
    placed = (P("depth", None, "scan", None), P(), P("scan", None), P("scan", None, None))
    return jax.shard_map(
        lambda *args: per_device(jnp.asarray(tab), *args),
        mesh=mesh,
        in_specs=placed,
        out_specs=(P("depth", None, "scan", None), P(None, "scan", "depth")),
        check_vma=False,
    )
```

```python
import math

import jax
import jax.numpy as jnp
import ml_dtypes
import numpy as np
from jax import lax
from jax.experimental import pallas as pl
from jax.experimental.pallas import tpu as pltpu
from jax.sharding import PartitionSpec as P

MESH = pl.DeviceIdType.MESH
N = 256
HALF = 128
TILE = 128
COLS = 384
SLICES = 16
PHASE_SCALE = 16.0
BF = jnp.bfloat16
F32 = jnp.float32
MATE = False


def real_form(table):
    return np.block([[table.real, table.imag], [-table.imag, table.real]])


def tables():
    n = np.arange(N)
    dft = np.exp(-2j * math.pi * (np.outer(n, n) % N) / N) / math.sqrt(N)
    q = ((n + HALF) % N - HALF) / N
    circulant = dft.conj() @ np.diag(np.exp(-1j * PHASE_SCALE * math.pi * q * q)) @ dft
    upper, lower = circulant[:HALF, :HALF], circulant[HALF:, :HALF]
    right = [
        real_form((upper + lower) / 2),
        real_form((upper - lower) / 2),
        real_form(dft[:HALF, 0::2]),
        real_form(dft[:HALF, 1::2]),
    ]
    full = np.stack(right + [t.T for t in right]).astype(np.float32)
    high = full.astype(ml_dtypes.bfloat16)
    low = (full - high.astype(np.float32)).astype(ml_dtypes.bfloat16)
    return np.stack([high, low], axis=1)


def dot(a, b):
    return jnp.dot(a, b, preferred_element_type=F32)


def one_hot(shape, hit):
    r = lax.broadcasted_iota(jnp.int32, shape, 0)
    c = lax.broadcasted_iota(jnp.int32, shape, 1)
    return jnp.where(hit(r, c), 1.0, 0.0).astype(BF)


def halves(x, axis):
    if axis == 0:
        return x[:HALF], x[HALF:]
    return x[:, :HALF], x[:, HALF:]


def butterfly(x, axis):
    first, second = halves(x, axis)
    return first + second, first - second


def join(a, b, axis):
    return jnp.concatenate([a, b], axis=axis)


def right_mul(x, tab, k):
    x = x.astype(BF)
    return dot(x, tab[k, 0]) + dot(x, tab[k, 1])


def left_mul(x, tab, k):
    x = x.astype(BF)
    return dot(tab[k, 0], x) + dot(tab[k, 1], x)


def columns_in(re, im, tab, k):
    sr, dr = butterfly(re, 1)
    si, di = butterfly(im, 1)
    a = right_mul(join(sr, si, 1), tab, k)
    b = right_mul(join(dr, di, 1), tab, k + 1)
    ar, ai = halves(a, 1)
    br, bi = halves(b, 1)
    return join(ar, br, 1), join(ai, bi, 1)


def rows_in(re, im, tab, k):
    sr, dr = butterfly(re, 0)
    si, di = butterfly(im, 0)
    a = left_mul(join(sr, si, 0), tab, k)
    b = left_mul(join(dr, di, 0), tab, k + 1)
    ar, ai = halves(a, 0)
    br, bi = halves(b, 0)
    return join(ar, br, 0), join(ai, bi, 0)


def rows_out(re, im, tab, k):
    re0, re1 = halves(re, 0)
    im0, im1 = halves(im, 0)
    a = left_mul(join(re0, im0, 0), tab, k)
    b = left_mul(join(re1, im1, 0), tab, k + 1)
    ar, ai = halves(a, 0)
    br, bi = halves(b, 0)
    return join(ar + br, ar - br, 0), join(ai + bi, ai - bi, 0)


def columns_out(re, im, tab, k):
    re0, re1 = halves(re, 1)
    im0, im1 = halves(im, 1)
    a = right_mul(join(re0, im0, 1), tab, k)
    b = right_mul(join(re1, im1, 1), tab, k + 1)
    ar, ai = halves(a, 1)
    br, bi = halves(b, 1)
    return join(ar + br, ar - br, 1), join(ai + bi, ai - bi, 1)


def propagate(re, im, tab, right, left):
    re, im = columns_in(re, im, tab, right)
    re, im = rows_in(re, im, tab, left)
    re, im = join(*butterfly(re, 0), 0), join(*butterfly(im, 0), 0)
    return join(*butterfly(re, 1), 1), join(*butterfly(im, 1), 1)


def remote(src, dst, send, recv, axis, index):
    return pltpu.make_async_remote_copy(
        src_ref=src,
        dst_ref=dst,
        send_sem=send,
        recv_sem=recv,
        device_id={axis: index},
        device_id_type=MESH,
    )


def kernel(
    off_hbm, obj_hbm, probe_hbm, int_hbm, tab_hbm,
    out_ref, probe_out,
    off_ref, obj, region, patch, held, waves, current, gout, gin, relay, rim, rim_in, tab, meas,
    turned, turned_in, pair, pair_in, spread, spread_in,
    load_sem, halo_send, halo_recv, patch_send, patch_recv, grad_send, grad_recv, relay_send, relay_recv,
    rim_send, rim_recv, turned_send, turned_recv, pair_send, pair_recv, spread_send, spread_recv,
):
    d = lax.axis_index("depth")
    m = lax.axis_index("scan")
    above, below = lax.rem(m + 31, 32), lax.rem(m + 1, 32)
    core = lax.rem(m, 2)
    place = m // 2
    x_lo = m // 16
    mate = m + 1 - 2 * core
    worker = [j * 8 + lax.rem(4 * core + 2 * j + x_lo, 8) for j in range(2)]
    mine = [d == w for w in worker]
    working = jnp.logical_or(mine[0], mine[1])
    helping = [d == j * 8 + lax.rem(4 * (1 - core) + 2 * j + x_lo, 8) for j in range(2)]

    off_copy = pltpu.make_async_copy(off_hbm, off_ref, load_sem.at[0])
    obj_copy = pltpu.make_async_copy(obj_hbm.at[0], obj, load_sem.at[1])
    tab_copy = pltpu.make_async_copy(tab_hbm, tab, load_sem.at[2])
    meas_copy = [pltpu.make_async_copy(int_hbm.at[j], meas, load_sem.at[3]) for j in range(2)]
    probe_copy = pltpu.make_async_copy(probe_hbm, current, load_sem.at[4])
    obj_copy.start()
    off_copy.start()

    for j in range(2):

        @pl.when(mine[j])
        def _():
            probe_copy.start()
            meas_copy[j].start()
            tab_copy.start()

    barrier = pltpu.get_barrier_semaphore()
    for t in (above, below):
        pl.semaphore_signal(barrier, inc=1, device_id={"scan": t}, device_id_type=MESH)
    for j in range(2):

        @pl.when(jnp.logical_not(mine[j]))
        def _():
            pl.semaphore_signal(barrier, inc=1, device_id={"depth": worker[j]}, device_id_type=MESH)

    def greet_place(k, c):
        @pl.when(k != place)
        def _():
            pl.semaphore_signal(barrier, inc=1, device_id={"scan": 2 * k + core}, device_id_type=MESH)

        return c

    @pl.when(working)
    def _():
        def greet(k, c):
            @pl.when(jnp.logical_and(k != worker[0], k != worker[1]))
            def _():
                pl.semaphore_signal(barrier, inc=1, device_id={"depth": k}, device_id_type=MESH)

            return c

        lax.fori_loop(0, SLICES, greet, 0)

    lax.fori_loop(0, 16, greet_place, 0)
    obj_copy.wait()
    region[1] = obj[...].astype(BF)
    off_copy.wait()
    row_off = [off_ref[j, 0] for j in range(2)]
    col_off = [off_ref[j, 1] for j in range(2)]

    @pl.when(working)
    def _():
        pl.semaphore_wait(barrier, 32)

    @pl.when(jnp.logical_not(working))
    def _():
        pl.semaphore_wait(barrier, 19)

    down = remote(region.at[1], region.at[0], halo_send.at[0], halo_recv.at[0], "scan", below)
    up = remote(region.at[1], region.at[2], halo_send.at[1], halo_recv.at[1], "scan", above)
    down.start()
    up.start()
    pick_cols = join(
        *[one_hot((COLS, N), lambda r, c, j=j: r == c + col_off[j]) for j in range(2)], 1
    )
    pick_rows = [one_hot((N, 3 * TILE), lambda r, c, j=j: c == r + row_off[j]) for j in range(2)]
    down.wait_recv()
    up.wait_recv()
    for c in range(2):
        strip = jnp.concatenate([region[t, c] for t in range(3)], axis=0)
        narrow = dot(strip, pick_cols).astype(BF)
        for j in range(2):
            patch[j, c] = dot(pick_rows[j], narrow[:, j * N : (j + 1) * N]).astype(BF)

    def patch_copy(j):
        return remote(patch.at[j], held.at[d], patch_send.at[j], patch_recv.at[d], "depth", worker[j])

    def patch_keep(j):
        return pltpu.make_async_copy(patch.at[j], held.at[d], patch_recv.at[d])

    for j in range(2):

        @pl.when(mine[j])
        def _():
            patch_keep(j).start()

        @pl.when(jnp.logical_not(mine[j]))
        def _():
            patch_copy(j).start()

    def turned_copy(j, k):
        rows = pl.ds(pl.multiple_of(k * 16, 16), 16)
        return remote(turned.at[rows], turned_in.at[j], turned_send.at[k], turned_recv.at[j], "depth", k)

    def turned_keep(j):
        rows = pl.ds(pl.multiple_of(d * 16, 16), 16)
        return pltpu.make_async_copy(turned.at[rows], turned_in.at[j], turned_recv.at[j])

    def relay_in(j, s):
        i = s - 8 * (1 - j)
        return remote(gout.at[s], relay.at[i], grad_send.at[s], relay_recv.at[i], "scan", mate)

    def relay_out(j, s):
        i = s - 8 * (1 - j)
        return pltpu.make_async_remote_copy(
            src_ref=relay.at[i],
            dst_ref=gin.at[j],
            send_sem=relay_send.at[i],
            recv_sem=grad_recv.at[j],
            device_id={"depth": s, "scan": mate},
            device_id_type=MESH,
        )

    def work(j):
        probe_copy.wait()
        meas_copy[j].wait()
        tab_copy.wait()
        even_odd = one_hot((N, N), lambda r, c: c == jnp.where(r < HALF, 2 * r, 2 * r - (N - 1)))
        even_odd_t = one_hot((N, N), lambda r, c: r == jnp.where(c < HALF, 2 * c, 2 * c - (N - 1)))
        measured = meas[...]
        high = measured.astype(BF)
        low = (measured - high.astype(F32)).astype(BF)
        meas[...] = dot(dot(even_odd, high).astype(BF), even_odd_t) + dot(
            dot(even_odd, low).astype(BF), even_odd_t
        )
        current[...] = current[...].astype(BF).astype(F32)

        def wait_patch(s):
            @pl.when(s == d)
            def _():
                patch_keep(j).wait()

            @pl.when(s != d)
            def _():
                remote(
                    patch.at[j], held.at[s], patch_send.at[j], patch_recv.at[s], "depth", worker[j]
                ).wait_recv()

        def exit_wave(s):
            wait_patch(s)
            wr, wi = current[0], current[1]
            waves[s, 0] = wr.astype(BF)
            waves[s, 1] = wi.astype(BF)
            pr, pi = held[s, 0].astype(F32), held[s, 1].astype(F32)
            return wr * pr - wi * pi, wr * pi + wi * pr

        def forward(s, carry):
            re, im = exit_wave(s)
            re, im = propagate(re, im, tab, 0, 4)
            current[0] = re
            current[1] = im
            return carry

        lax.fori_loop(0, SLICES - 1, forward, 0)
        re, im = exit_wave(SLICES - 1)
        re, im = columns_in(re, im, tab, 2)
        re, im = rows_in(re, im, tab, 6)
        misfit = re * re + im * im - meas[...]
        re, im = rows_out(misfit * re, misfit * im, tab, 2)
        re, im = columns_out(re, im, tab, 6)
        current[0] = re
        current[1] = im

        def grad_copy(s):
            return remote(gout.at[s], gin.at[j], grad_send.at[s], grad_recv.at[j], "depth", s)

        def grad_keep(s):
            return pltpu.make_async_copy(gout.at[s], gin.at[j], grad_recv.at[j])

        def across(s):
            return jnp.logical_and(MATE, s // 8 != j)

        def through(s):
            gr, gi = current[0], current[1]
            wr, wi = waves[s, 0].astype(F32), waves[s, 1].astype(F32)
            gout[s, 0] = (wr * gr + wi * gi).astype(BF)
            gout[s, 1] = (wr * gi - wi * gr).astype(BF)

            @pl.when(s == d)
            def _():
                grad_keep(s).start()

            @pl.when(across(s))
            def _():
                relay_in(j, s).start()

            @pl.when(jnp.logical_and(s != d, jnp.logical_not(across(s))))
            def _():
                grad_copy(s).start()

            pr, pi = held[s, 0].astype(F32), held[s, 1].astype(F32)
            return pr * gr + pi * gi, pr * gi - pi * gr

        def backward(i, carry):
            re, im = through(SLICES - 1 - i)
            re, im = propagate(re, im, tab, 4, 0)
            current[0] = re
            current[1] = im
            return carry

        lax.fori_loop(0, SLICES - 1, backward, 0)
        re, im = through(0)
        sums = []
        for c, part in enumerate((re, im)):
            chosen = one_hot(
                (N, 2 * N),
                lambda r, l, c=c: l
                == lax.rem(r // 8, 2) * N + (r // 16) * 16 + c * 8 + lax.rem(r, 8),
            )
            sums.append(dot(jnp.transpose(part).astype(BF), chosen))
        turned[...] = (sums[0] + sums[1]).astype(BF)
        turned_keep(j).start()

        def turn(k, carry):
            @pl.when(k != d)
            def _():
                turned_copy(j, k).start()

            return carry

        lax.fori_loop(0, SLICES, turn, 0)

    for j in range(2):

        @pl.when(mine[j])
        def _():
            work(j)

        @pl.when(jnp.logical_and(MATE, helping[j]))
        def _():
            def pass_on(i, carry):
                s = 8 * (1 - j) + 7 - i
                relay_in(j, s).wait_recv()
                relay_out(j, s).start()
                return carry

            lax.fori_loop(0, 8, pass_on, 0)

    for j in range(2):

        @pl.when(jnp.logical_not(mine[j]))
        def _():
            remote(gout.at[0], gin.at[j], grad_send.at[0], grad_recv.at[j], "depth", d).wait_recv()

        @pl.when(mine[j])
        def _():
            pltpu.make_async_copy(gout.at[d], gin.at[j], grad_recv.at[j]).wait()

    put_cols = [one_hot((N, COLS), lambda r, c, j=j: c == r + col_off[j]) for j in range(2)]
    put_rows = join(
        *[one_hot((3 * TILE, N), lambda r, c, j=j: r == c + row_off[j]) for j in range(2)], 1
    )
    for c in range(2):
        wide = join(*[dot(gin[j, c], put_cols[j]).astype(BF) for j in range(2)], 0)
        total = dot(put_rows, wide)
        rim[0, c] = total[:TILE].astype(BF)
        rim[1, c] = total[2 * TILE :].astype(BF)
        out_ref[0, c] = total[TILE : 2 * TILE]
    to_above = remote(rim.at[0], rim_in.at[0], rim_send.at[0], rim_recv.at[0], "scan", above)
    to_below = remote(rim.at[1], rim_in.at[1], rim_send.at[1], rim_recv.at[1], "scan", below)
    to_above.start()
    to_below.start()

    for j in range(2):

        @pl.when(mine[j])
        def _():
            turned_keep(j).wait()

        @pl.when(jnp.logical_not(mine[j]))
        def _():
            turned_copy(j, d).wait_recv()

    both = turned_in[0].astype(F32) + turned_in[1].astype(F32)
    for h in range(2):
        pair[h] = both[:, h * N : (h + 1) * N].astype(BF)
    to_mate = remote(pair.at[1 - core], pair_in, pair_send, pair_recv, "scan", mate)
    to_mate.start()
    to_mate.wait_recv()
    four = pair[core].astype(F32) + pair_in[...].astype(F32)
    for h in range(2):
        spread[h] = four[:, h * HALF : (h + 1) * HALF].astype(BF)

    def spread_copy(k):
        return remote(
            spread.at[k // 8], spread_in.at[place], spread_send.at[k], spread_recv.at[place], "scan", 2 * k + core
        )

    def spread_wait(k):
        return remote(
            spread.at[k // 8], spread_in.at[k], spread_send.at[k], spread_recv.at[k], "scan", 2 * k + core
        )

    def send_spread(k, carry):
        @pl.when(k != place)
        def _():
            spread_copy(k).start()

        return carry

    lax.fori_loop(0, 16, send_spread, 0)
    spread_in[place] = spread[x_lo]
    to_above.wait_recv()
    to_below.wait_recv()
    out_ref[0] = out_ref[0] + rim_in[0].astype(F32) + rim_in[1].astype(F32)

    def take_spread(k, carry):
        @pl.when(k != place)
        def _():
            spread_wait(k).wait_recv()

        return carry

    lax.fori_loop(0, 16, take_spread, 0)
    everything = spread_in[0].astype(F32)
    for k in range(1, 16):
        everything = everything + spread_in[k].astype(F32)
    own = one_hot((16, HALF), lambda r, l: l == lax.rem(place, 8) * 16 + r)
    top = everything.astype(BF)
    rest = (everything - top.astype(F32)).astype(BF)
    lanes = (((1,), (1,)), ((), ()))
    final = lax.dot_general(own, top, lanes, preferred_element_type=F32) + lax.dot_general(
        own, rest, lanes, preferred_element_type=F32
    )
    probe_out[0] = final[:8]
    probe_out[1] = final[8:]

    down.wait_send()
    up.wait_send()
    to_above.wait_send()
    to_below.wait_send()
    to_mate.wait_send()

    def sent_spread(k, carry):
        @pl.when(k != place)
        def _():
            spread_copy(k).wait_send()

        return carry

    lax.fori_loop(0, 16, sent_spread, 0)
    for j in range(2):

        @pl.when(jnp.logical_not(mine[j]))
        def _():
            patch_copy(j).wait_send()

        @pl.when(jnp.logical_and(MATE, helping[j]))
        def _():
            def passed(i, carry):
                relay_out(j, 8 * (1 - j) + 7 - i).wait_send()
                return carry

            lax.fori_loop(0, 8, passed, 0)

        @pl.when(mine[j])
        def _():
            def sent(s, carry):
                @pl.when(s != d)
                def _():
                    remote(gout.at[s], gin.at[j], grad_send.at[s], grad_recv.at[j], "depth", s).wait_send()
                    turned_copy(j, s).wait_send()

                return carry

            lax.fori_loop(0, SLICES, sent, 0)


def per_device(tab, object_slices, probe, offsets, intensity):
    vmem = pl.BlockSpec(memory_space=pltpu.VMEM)
    anywhere = pl.BlockSpec(memory_space=pl.ANY)
    plane = (2, N, N)
    strip = (2, TILE, COLS)
    dma = pltpu.SemaphoreType.DMA
    return pl.pallas_call(
        kernel,
        out_shape=(
            jax.ShapeDtypeStruct(object_slices.shape, F32),
            jax.ShapeDtypeStruct((2, 8, 16), F32),
        ),
        in_specs=[anywhere] * 5,
        out_specs=(vmem, vmem),
        scratch_shapes=[
            pltpu.SMEM(offsets.shape, jnp.int32),
            pltpu.VMEM(strip, F32),
            pltpu.VMEM((3, *strip), BF),
            pltpu.VMEM((2, *plane), BF),
            pltpu.VMEM((SLICES, *plane), BF),
            pltpu.VMEM((SLICES, *plane), BF),
            pltpu.VMEM(plane, F32),
            pltpu.VMEM((SLICES, *plane), BF),
            pltpu.VMEM((2, *plane), BF),
            pltpu.VMEM((8, *plane), BF),
            pltpu.VMEM((2, *strip), BF),
            pltpu.VMEM((2, *strip), BF),
            pltpu.VMEM((8, 2, N, N), BF),
            pltpu.VMEM((N, N), F32),
            pltpu.VMEM((N, 2 * N), BF),
            pltpu.VMEM((2, 16, 2 * N), BF),
            pltpu.VMEM((2, 16, N), BF),
            pltpu.VMEM((16, N), BF),
            pltpu.VMEM((2, 16, HALF), BF),
            pltpu.VMEM((16, 16, HALF), BF),
            dma((5,)),
            dma((2,)),
            dma((2,)),
            dma((2,)),
            dma((SLICES,)),
            dma((SLICES,)),
            dma((2,)),
            dma((8,)),
            dma((8,)),
            dma((2,)),
            dma((2,)),
            dma((SLICES,)),
            dma((2,)),
            dma,
            dma,
            dma((16,)),
            dma((16,)),
        ],
        compiler_params=pltpu.CompilerParams(
            collective_id=0, has_side_effects=True, vmem_limit_bytes=60 << 20
        ),
        name="ptychography_chains",
    )(offsets, object_slices, probe, intensity, tab)


def solution(mesh):
    tab = tables()
    placed = (P("depth", None, "scan", None), P(), P("scan", None), P("scan", None, None))
    return jax.shard_map(
        lambda *args: per_device(jnp.asarray(tab), *args),
        mesh=mesh,
        in_specs=placed,
        out_specs=(P("depth", None, "scan", None), P(None, "scan", "depth")),
        check_vma=False,
    )
```

```python
import math

import jax
import jax.numpy as jnp
import ml_dtypes
import numpy as np
from jax import lax
from jax.experimental import pallas as pl
from jax.experimental.pallas import tpu as pltpu
from jax.sharding import PartitionSpec as P

MESH = pl.DeviceIdType.MESH
N = 256
HALF = 128
TILE = 128
COLS = 384
SLICES = 16
PHASE_SCALE = 16.0
BF = jnp.bfloat16
F32 = jnp.float32
IN_STEPS = ((1, 7), (1, 7))
OUT_STEPS = ((), ())
BENCH = (4, 2, 0, 0)


def real_form(table):
    return np.block([[table.real, table.imag], [-table.imag, table.real]])


def tables():
    n = np.arange(N)
    dft = np.exp(-2j * math.pi * (np.outer(n, n) % N) / N) / math.sqrt(N)
    q = ((n + HALF) % N - HALF) / N
    circulant = dft.conj() @ np.diag(np.exp(-1j * PHASE_SCALE * math.pi * q * q)) @ dft
    upper, lower = circulant[:HALF, :HALF], circulant[HALF:, :HALF]
    right = [
        real_form((upper + lower) / 2),
        real_form((upper - lower) / 2),
        real_form(dft[:HALF, 0::2]),
        real_form(dft[:HALF, 1::2]),
    ]
    full = np.stack(right + [t.T for t in right]).astype(np.float32)
    high = full.astype(ml_dtypes.bfloat16)
    low = (full - high.astype(np.float32)).astype(ml_dtypes.bfloat16)
    return np.stack([high, low], axis=1)


def dot(a, b):
    return jnp.dot(a, b, preferred_element_type=F32)


def one_hot(shape, hit):
    r = lax.broadcasted_iota(jnp.int32, shape, 0)
    c = lax.broadcasted_iota(jnp.int32, shape, 1)
    return jnp.where(hit(r, c), 1.0, 0.0).astype(BF)


def halves(x, axis):
    if axis == 0:
        return x[:HALF], x[HALF:]
    return x[:, :HALF], x[:, HALF:]


def butterfly(x, axis):
    first, second = halves(x, axis)
    return first + second, first - second


def join(a, b, axis):
    return jnp.concatenate([a, b], axis=axis)


def right_mul(x, tab, k):
    x = x.astype(BF)
    return dot(x, tab[k, 0]) + dot(x, tab[k, 1])


def left_mul(x, tab, k):
    x = x.astype(BF)
    return dot(tab[k, 0], x) + dot(tab[k, 1], x)


def columns_in(re, im, tab, k):
    sr, dr = butterfly(re, 1)
    si, di = butterfly(im, 1)
    a = right_mul(join(sr, si, 1), tab, k)
    b = right_mul(join(dr, di, 1), tab, k + 1)
    ar, ai = halves(a, 1)
    br, bi = halves(b, 1)
    return join(ar, br, 1), join(ai, bi, 1)


def rows_in(re, im, tab, k):
    sr, dr = butterfly(re, 0)
    si, di = butterfly(im, 0)
    a = left_mul(join(sr, si, 0), tab, k)
    b = left_mul(join(dr, di, 0), tab, k + 1)
    ar, ai = halves(a, 0)
    br, bi = halves(b, 0)
    return join(ar, br, 0), join(ai, bi, 0)


def rows_out(re, im, tab, k):
    re0, re1 = halves(re, 0)
    im0, im1 = halves(im, 0)
    a = left_mul(join(re0, im0, 0), tab, k)
    b = left_mul(join(re1, im1, 0), tab, k + 1)
    ar, ai = halves(a, 0)
    br, bi = halves(b, 0)
    return join(ar + br, ar - br, 0), join(ai + bi, ai - bi, 0)


def columns_out(re, im, tab, k):
    re0, re1 = halves(re, 1)
    im0, im1 = halves(im, 1)
    a = right_mul(join(re0, im0, 1), tab, k)
    b = right_mul(join(re1, im1, 1), tab, k + 1)
    ar, ai = halves(a, 1)
    br, bi = halves(b, 1)
    return join(ar + br, ar - br, 1), join(ai + bi, ai - bi, 1)


def propagate(re, im, tab, right, left):
    re, im = columns_in(re, im, tab, right)
    re, im = rows_in(re, im, tab, left)
    re, im = join(*butterfly(re, 0), 0), join(*butterfly(im, 0), 0)
    return join(*butterfly(re, 1), 1), join(*butterfly(im, 1), 1)


def keep(hit, x):
    return jnp.where(hit, x, jnp.zeros_like(x))


def rotated_columns(x, off):
    first, middle, last = x[:, :HALF], x[:, HALF:N], x[:, N:]
    lane = lax.broadcasted_iota(jnp.int32, first.shape, 1)
    return join(jnp.where(lane < off, last, first), middle, 1)


def object_columns(x, off):
    first = x[:, :HALF]
    lane = lax.broadcasted_iota(jnp.int32, first.shape, 1)
    return jnp.concatenate([keep(lane >= off, first), x[:, HALF:], keep(lane < off, first)], axis=1)


def rows_below(shape, off):
    return lax.broadcasted_iota(jnp.int32, shape, 0) < off


def behind(x, off):
    return lax.rem(x - off + N, N)


def remote(src, dst, send, recv, axis, index):
    return pltpu.make_async_remote_copy(
        src_ref=src,
        dst_ref=dst,
        send_sem=send,
        recv_sem=recv,
        device_id={axis: index},
        device_id_type=MESH,
    )


def kernel(
    off_hbm, obj_hbm, probe_hbm, int_hbm, tab_hbm,
    out_ref, probe_out,
    off_ref, obj, tile, halo, patch, held, waves, current, gout, gin, detour, returned, rim, rim_in, tab, meas,
    turned, turned_in, pair, pair_in, spread, spread_in,
    load_sem, halo_send, halo_recv, patch_send, patch_recv, grad_send, grad_recv, detour_send, detour_recv, returned_send, returned_recv,
    rim_send, rim_recv, turned_send, turned_recv, pair_send, pair_recv, spread_send, spread_recv,
):
    d = lax.axis_index("depth")
    m = lax.axis_index("scan")
    above, below = lax.rem(m + 31, 32), lax.rem(m + 1, 32)
    core = lax.rem(m, 2)
    place = m // 2
    x_lo = m // 16
    mate = m + 1 - 2 * core
    side, z = d // 8, lax.rem(d, 8)
    bench = [lax.rem(BENCH[0] * core + BENCH[1] * j + BENCH[2] * x_lo + BENCH[3], 8) for j in range(2)]
    worker = [j * 8 + bench[j] for j in range(2)]

    def steps_in(place_z, j, steps):
        hit = jnp.bool_(False)
        for step in steps:
            hit = jnp.logical_or(hit, place_z == lax.rem(bench[j] + step, 8))
        return hit

    detoured = [jnp.logical_and(side != j, steps_in(z, j, IN_STEPS[j])) for j in range(2)]
    mine = [d == w for w in worker]
    working = jnp.logical_or(mine[0], mine[1])

    def either(a, b):
        return jnp.logical_or(a, b)

    carries = [jnp.logical_and(side == j, steps_in(z, j, IN_STEPS[j])) for j in range(2)]
    hub = [d == (1 - j) * 8 + bench[j] for j in range(2)]
    handed = [jnp.logical_and(side != j, steps_in(z, j, OUT_STEPS[j])) for j in range(2)]

    def one(hit):
        return jnp.where(hit, 1, 0)

    greetings = jnp.where(working, 18, 19) + one(either(*detoured)) + sum(len(OUT_STEPS[j]) * one(hub[j]) for j in range(2))
    off_copy = pltpu.make_async_copy(off_hbm, off_ref, load_sem.at[0])
    obj_copy = pltpu.make_async_copy(obj_hbm.at[0], obj, load_sem.at[1])
    tab_copy = pltpu.make_async_copy(tab_hbm, tab, load_sem.at[2])
    meas_copy = [pltpu.make_async_copy(int_hbm.at[j], meas, load_sem.at[3]) for j in range(2)]
    probe_copy = pltpu.make_async_copy(probe_hbm, current, load_sem.at[4])
    obj_copy.start()
    off_copy.start()

    for j in range(2):

        @pl.when(mine[j])
        def _():
            probe_copy.start()
            meas_copy[j].start()
            tab_copy.start()

    barrier = pltpu.get_barrier_semaphore()

    @pl.when(working)
    def _():
        def greet(k, c):
            @pl.when(k != d)
            def _():
                pl.semaphore_signal(barrier, inc=1, device_id={"depth": k}, device_id_type=MESH)

            return c

        lax.fori_loop(0, SLICES, greet, 0)

    for t in (above, below):
        pl.semaphore_signal(barrier, inc=1, device_id={"scan": t}, device_id_type=MESH)
    @pl.when(either(*carries))
    def _():
        pl.semaphore_signal(barrier, inc=1, device_id={"depth": lax.rem(d + 8, 16)}, device_id_type=MESH)

    for j in range(2):

        @pl.when(handed[j])
        def _():
            centre = (1 - j) * 8 + bench[j]
            pl.semaphore_signal(barrier, inc=1, device_id={"depth": centre}, device_id_type=MESH)

    def greet_place(k, c):
        @pl.when(k != place)
        def _():
            pl.semaphore_signal(barrier, inc=1, device_id={"scan": 2 * k + core}, device_id_type=MESH)

        return c

    lax.fori_loop(0, 16, greet_place, 0)
    obj_copy.wait()
    tile[...] = obj[...].astype(BF)
    off_copy.wait()
    row_off = [off_ref[j, 0] for j in range(2)]
    col_off = [off_ref[j, 1] for j in range(2)]

    pl.semaphore_wait(barrier, greetings)

    down = remote(tile, halo.at[0], halo_send.at[0], halo_recv.at[0], "scan", below)
    up = remote(tile, halo.at[1], halo_send.at[1], halo_recv.at[1], "scan", above)
    down.start()
    up.start()

    def patch_copy(j, h):
        return remote(
            patch.at[j, h], held.at[d, h], patch_send.at[j, h], patch_recv.at[h, d], "depth", worker[j]
        )

    def patch_keep(j, h):
        return pltpu.make_async_copy(patch.at[j, h], held.at[d, h], patch_recv.at[h, d])

    def detour_in(j, h, to):
        return remote(patch.at[j, h], detour.at[h], patch_send.at[j, h], detour_recv.at[h], "depth", to)

    def detour_out(j, h):
        source = d + 8 - 16 * j
        return remote(
            detour.at[h], held.at[source, h], detour_send.at[h], patch_recv.at[h, source], "depth", worker[j]
        )

    def hand_in(h):
        for j in range(2):

            @pl.when(mine[j])
            def _():
                patch_keep(j, h).start()

            @pl.when(jnp.logical_not(jnp.logical_or(mine[j], detoured[j])))
            def _():
                patch_copy(j, h).start()

            @pl.when(detoured[j])
            def _():
                detour_in(j, h, d - 8 + 16 * j).start()

    for j in range(2):
        for c in range(2):
            patch[j, 1, c] = rotated_columns(obj[c], col_off[j]).astype(BF)
    hand_in(1)
    down.wait_recv()
    up.wait_recv()
    for c in range(2):
        over, under = halo[0, c].astype(F32), halo[1, c].astype(F32)
        for j in range(2):
            rows = jnp.where(rows_below(over.shape, row_off[j]), under, over)
            patch[j, 0, c] = rotated_columns(rows, col_off[j]).astype(BF)
    hand_in(0)

    def turned_copy(j, k):
        rows = pl.ds(pl.multiple_of(k * 16, 16), 16)
        return remote(turned.at[rows], turned_in.at[j], turned_send.at[k], turned_recv.at[j], "depth", k)

    def turned_keep(j):
        rows = pl.ds(pl.multiple_of(d * 16, 16), 16)
        return pltpu.make_async_copy(turned.at[rows], turned_in.at[j], turned_recv.at[j])

    for j in range(2):

        @pl.when(carries[j])
        def _():
            for h in (1, 0):
                detour_in(j, h, d).wait_recv()
                detour_out(j, h).start()

    def return_in(j, s):
        i = lax.rem(s, 8)
        return remote(
            gout.at[s], returned.at[i], grad_send.at[s], returned_recv.at[i], "depth", (1 - j) * 8 + bench[j]
        )

    def return_out(j, i):
        return remote(
            returned.at[i], gin.at[j], returned_send.at[i], grad_recv.at[j], "depth", (1 - j) * 8 + i
        )

    def work(j):
        probe_copy.wait()
        meas_copy[j].wait()
        tab_copy.wait()
        even_odd = one_hot((N, N), lambda r, c: c == jnp.where(r < HALF, 2 * r, 2 * r - (N - 1)))
        even_odd_t = one_hot((N, N), lambda r, c: r == jnp.where(c < HALF, 2 * c, 2 * c - (N - 1)))
        measured = meas[...]
        high = measured.astype(BF)
        low = (measured - high.astype(F32)).astype(BF)
        meas[...] = dot(dot(even_odd, high).astype(BF), even_odd_t) + dot(
            dot(even_odd, low).astype(BF), even_odd_t
        )
        turn_rows = one_hot((N, N), lambda r, c: c == behind(r, row_off[j]))
        turn_cols = one_hot((N, N), lambda r, c: r == behind(c, col_off[j]))
        for c in range(2):
            current[c] = dot(dot(turn_rows, current[c].astype(BF)).astype(BF), turn_cols)

        def wait_patch(s):
            for h in range(2):

                @pl.when(s == d)
                def _():
                    patch_keep(j, h).wait()

                @pl.when(s != d)
                def _():
                    remote(
                        patch.at[j, h], held.at[s, h], patch_send.at[j, h], patch_recv.at[h, s], "depth", worker[j]
                    ).wait_recv()

        def held_patch(s):
            return [join(held[s, 0, c], held[s, 1, c], 0).astype(F32) for c in range(2)]

        def exit_wave(s):
            wait_patch(s)
            wr, wi = current[0], current[1]
            waves[s, 0] = wr.astype(BF)
            waves[s, 1] = wi.astype(BF)
            pr, pi = held_patch(s)
            return wr * pr - wi * pi, wr * pi + wi * pr

        def forward(s, carry):
            re, im = exit_wave(s)
            re, im = propagate(re, im, tab, 0, 4)
            current[0] = re
            current[1] = im
            return carry

        lax.fori_loop(0, SLICES - 1, forward, 0)
        re, im = exit_wave(SLICES - 1)
        re, im = columns_in(re, im, tab, 2)
        re, im = rows_in(re, im, tab, 6)
        misfit = re * re + im * im - meas[...]
        re, im = rows_out(misfit * re, misfit * im, tab, 2)
        re, im = columns_out(re, im, tab, 6)
        current[0] = re
        current[1] = im

        def grad_copy(s):
            return remote(gout.at[s], gin.at[j], grad_send.at[s], grad_recv.at[j], "depth", s)

        def grad_keep(s):
            return pltpu.make_async_copy(gout.at[s], gin.at[j], grad_recv.at[j])

        def across(s):
            return jnp.logical_and(s // 8 != j, steps_in(lax.rem(s, 8), j, OUT_STEPS[j]))

        def through(s):
            gr, gi = current[0], current[1]
            wr, wi = waves[s, 0].astype(F32), waves[s, 1].astype(F32)
            for c, product in enumerate((wr * gr + wi * gi, wr * gi - wi * gr)):
                for h, rows in enumerate(halves(product.astype(BF), 0)):
                    gout[s, h, c] = rows

            @pl.when(s == d)
            def _():
                grad_keep(s).start()

            @pl.when(across(s))
            def _():
                return_in(j, s).start()

            @pl.when(jnp.logical_and(s != d, jnp.logical_not(across(s))))
            def _():
                grad_copy(s).start()

            pr, pi = held_patch(s)
            return pr * gr + pi * gi, pr * gi - pi * gr

        def backward(i, carry):
            re, im = through(SLICES - 1 - i)
            re, im = propagate(re, im, tab, 4, 0)
            current[0] = re
            current[1] = im
            return carry

        lax.fori_loop(0, SLICES - 1, backward, 0)
        re, im = through(0)
        sums = []
        back_cols = one_hot((N, N), lambda r, c: c == behind(r, col_off[j]))
        for c, part in enumerate((re, im)):

            def lane_of(row, c=c):
                return lax.rem(row // 8, 2) * N + (row // 16) * 16 + c * 8 + lax.rem(row, 8)

            chosen = one_hot((N, 2 * N), lambda r, l: l == lane_of(behind(r, row_off[j])))
            straight = jnp.transpose(dot(part.astype(BF), back_cols))
            sums.append(dot(straight.astype(BF), chosen))
        turned[...] = (sums[0] + sums[1]).astype(BF)
        turned_keep(j).start()

        def turn(k, carry):
            @pl.when(k != d)
            def _():
                turned_copy(j, k).start()

            return carry

        lax.fori_loop(0, SLICES, turn, 0)

    for j in range(2):

        @pl.when(mine[j])
        def _():
            work(j)

        @pl.when(hub[j])
        def _():
            def pass_on(k, carry):
                i = 7 - k

                @pl.when(steps_in(i, j, OUT_STEPS[j]))
                def _():
                    return_in(j, (1 - j) * 8 + i).wait_recv()
                    return_out(j, i).start()

                return carry

            lax.fori_loop(0, 8, pass_on, 0)

    for j in range(2):

        @pl.when(jnp.logical_not(mine[j]))
        def _():
            remote(gout.at[0], gin.at[j], grad_send.at[0], grad_recv.at[j], "depth", d).wait_recv()

        @pl.when(mine[j])
        def _():
            pltpu.make_async_copy(gout.at[d], gin.at[j], grad_recv.at[j]).wait()

    for c in range(2):
        own, over, under = 0.0, 0.0, 0.0
        for j in range(2):
            own = own + object_columns(gin[j, 1, c].astype(F32), col_off[j])
            edge = object_columns(gin[j, 0, c].astype(F32), col_off[j])
            low = rows_below(edge.shape, row_off[j])
            over = over + keep(jnp.logical_not(low), edge)
            under = under + keep(low, edge)
        out_ref[0, c] = own
        rim[0, c] = over.astype(BF)
        rim[1, c] = under.astype(BF)
    to_above = remote(rim.at[0], rim_in.at[0], rim_send.at[0], rim_recv.at[0], "scan", above)
    to_below = remote(rim.at[1], rim_in.at[1], rim_send.at[1], rim_recv.at[1], "scan", below)
    to_above.start()
    to_below.start()

    for j in range(2):

        @pl.when(mine[j])
        def _():
            turned_keep(j).wait()

        @pl.when(jnp.logical_not(mine[j]))
        def _():
            turned_copy(j, d).wait_recv()

    both = turned_in[0].astype(F32) + turned_in[1].astype(F32)
    for h in range(2):
        pair[h] = both[:, h * N : (h + 1) * N].astype(BF)
    to_mate = remote(pair.at[1 - core], pair_in, pair_send, pair_recv, "scan", mate)
    to_mate.start()
    to_mate.wait_recv()
    four = pair[core].astype(F32) + pair_in[...].astype(F32)
    for h in range(2):
        spread[h] = four[:, h * HALF : (h + 1) * HALF].astype(BF)

    def spread_copy(k):
        return remote(
            spread.at[k // 8], spread_in.at[place], spread_send.at[k], spread_recv.at[place], "scan", 2 * k + core
        )

    def spread_wait(k):
        return remote(
            spread.at[k // 8], spread_in.at[k], spread_send.at[k], spread_recv.at[k], "scan", 2 * k + core
        )

    def send_spread(k, carry):
        @pl.when(k != place)
        def _():
            spread_copy(k).start()

        return carry

    lax.fori_loop(0, 16, send_spread, 0)
    spread_in[place] = spread[x_lo]
    to_above.wait_recv()
    to_below.wait_recv()
    out_ref[0] = out_ref[0] + rim_in[0].astype(F32) + rim_in[1].astype(F32)

    def take_spread(k, carry):
        @pl.when(k != place)
        def _():
            spread_wait(k).wait_recv()

        return carry

    lax.fori_loop(0, 16, take_spread, 0)
    everything = spread_in[0].astype(F32)
    for k in range(1, 16):
        everything = everything + spread_in[k].astype(F32)
    own = one_hot((16, HALF), lambda r, l: l == lax.rem(place, 8) * 16 + r)
    top = everything.astype(BF)
    rest = (everything - top.astype(F32)).astype(BF)
    lanes = (((1,), (1,)), ((), ()))
    final = lax.dot_general(own, top, lanes, preferred_element_type=F32) + lax.dot_general(
        own, rest, lanes, preferred_element_type=F32
    )
    probe_out[0] = final[:8]
    probe_out[1] = final[8:]

    down.wait_send()
    up.wait_send()
    to_above.wait_send()
    to_below.wait_send()
    to_mate.wait_send()

    def sent_spread(k, carry):
        @pl.when(k != place)
        def _():
            spread_copy(k).wait_send()

        return carry

    lax.fori_loop(0, 16, sent_spread, 0)
    for j in range(2):

        @pl.when(jnp.logical_not(mine[j]))
        def _():
            patch_copy(j, 0).wait_send()
            patch_copy(j, 1).wait_send()

        @pl.when(carries[j])
        def _():
            for h in range(2):
                detour_out(j, h).wait_send()

        @pl.when(hub[j])
        def _():
            def passed(i, carry):
                @pl.when(steps_in(i, j, OUT_STEPS[j]))
                def _():
                    return_out(j, i).wait_send()

                return carry

            lax.fori_loop(0, 8, passed, 0)

        @pl.when(mine[j])
        def _():
            def sent(s, carry):
                @pl.when(s != d)
                def _():
                    remote(gout.at[s], gin.at[j], grad_send.at[s], grad_recv.at[j], "depth", s).wait_send()
                    turned_copy(j, s).wait_send()

                return carry

            lax.fori_loop(0, SLICES, sent, 0)


def results(grad_ref, probe_ref, out_ref, probe_out):
    out_ref[...] = grad_ref[...]
    probe_out[...] = probe_ref[...]


def per_device(tab, object_slices, probe, offsets, intensity):
    vmem = pl.BlockSpec(memory_space=pltpu.VMEM)
    anywhere = pl.BlockSpec(memory_space=pl.ANY)
    plane = (2, N, N)
    strip = (2, TILE, COLS)
    parts = (2, 2, HALF, N)
    dma = pltpu.SemaphoreType.DMA
    outs = (
        jax.ShapeDtypeStruct(object_slices.shape, F32),
        jax.ShapeDtypeStruct((2, 8, 16), F32),
    )
    grads = pl.pallas_call(
        kernel,
        out_shape=outs,
        in_specs=[anywhere] * 5,
        out_specs=(vmem, vmem),
        scratch_shapes=[
            pltpu.SMEM(offsets.shape, jnp.int32),
            pltpu.VMEM(strip, F32),
            pltpu.VMEM(strip, BF),
            pltpu.VMEM((2, *strip), BF),
            pltpu.VMEM((2, *parts), BF),
            pltpu.VMEM((SLICES, *parts), BF),
            pltpu.VMEM((SLICES, *plane), BF),
            pltpu.VMEM(plane, F32),
            pltpu.VMEM((SLICES, *parts), BF),
            pltpu.VMEM((2, *parts), BF),
            pltpu.VMEM(parts, BF),
            pltpu.VMEM((8, *parts), BF),
            pltpu.VMEM((2, *strip), BF),
            pltpu.VMEM((2, *strip), BF),
            pltpu.VMEM((8, 2, N, N), BF),
            pltpu.VMEM((N, N), F32),
            pltpu.VMEM((N, 2 * N), BF),
            pltpu.VMEM((2, 16, 2 * N), BF),
            pltpu.VMEM((2, 16, N), BF),
            pltpu.VMEM((16, N), BF),
            pltpu.VMEM((2, 16, HALF), BF),
            pltpu.VMEM((16, 16, HALF), BF),
            dma((5,)),
            dma((2,)),
            dma((2,)),
            dma((2, 2)),
            dma((2, SLICES)),
            dma((SLICES,)),
            dma((2,)),
            dma((2,)),
            dma((2,)),
            dma((8,)),
            dma((8,)),
            dma((2,)),
            dma((2,)),
            dma((SLICES,)),
            dma((2,)),
            dma,
            dma,
            dma((16,)),
            dma((16,)),
        ],
        compiler_params=pltpu.CompilerParams(
            collective_id=0, has_side_effects=True, vmem_limit_bytes=60 << 20
        ),
        name="ptychography_chains",
    )(offsets, object_slices, probe, intensity, tab)
    return pl.pallas_call(
        results,
        out_shape=outs,
        in_specs=[vmem] * 2,
        out_specs=(vmem, vmem),
        name="results",
    )(*grads)


def solution(mesh):
    tab = tables()
    placed = (P("depth", None, "scan", None), P(), P("scan", None), P("scan", None, None))
    return jax.shard_map(
        lambda *args: per_device(jnp.asarray(tab), *args),
        mesh=mesh,
        in_specs=placed,
        out_specs=(P("depth", None, "scan", None), P(None, "scan", "depth")),
        check_vma=False,
    )
```

```python
import math

import jax
import jax.numpy as jnp
import ml_dtypes
import numpy as np
from jax import lax
from jax.experimental import pallas as pl
from jax.experimental.pallas import tpu as pltpu
from jax.sharding import PartitionSpec as P

MESH = pl.DeviceIdType.MESH
N = 256
HALF = 128
TILE = 128
COLS = 384
SLICES = 16
PHASE_SCALE = 16.0
BF = jnp.bfloat16
F32 = jnp.float32
IN_STEPS = ((), (1, 7))
OUT_STEPS = ((), ())
LATE = (4, 8)
BENCH = (4, 2, 0)


def real_form(table):
    return np.block([[table.real, table.imag], [-table.imag, table.real]])


def tables():
    n = np.arange(N)
    dft = np.exp(-2j * math.pi * (np.outer(n, n) % N) / N) / math.sqrt(N)
    q = ((n + HALF) % N - HALF) / N
    circulant = dft.conj() @ np.diag(np.exp(-1j * PHASE_SCALE * math.pi * q * q)) @ dft
    upper, lower = circulant[:HALF, :HALF], circulant[HALF:, :HALF]
    right = [
        real_form((upper + lower) / 2),
        real_form((upper - lower) / 2),
        real_form(dft[:HALF, 0::2]),
        real_form(dft[:HALF, 1::2]),
    ]
    full = np.stack(right + [t.T for t in right]).astype(np.float32)
    high = full.astype(ml_dtypes.bfloat16)
    low = (full - high.astype(np.float32)).astype(ml_dtypes.bfloat16)
    return np.stack([high, low], axis=1)


def dot(a, b):
    return jnp.dot(a, b, preferred_element_type=F32)


def one_hot(shape, hit):
    r = lax.broadcasted_iota(jnp.int32, shape, 0)
    c = lax.broadcasted_iota(jnp.int32, shape, 1)
    return jnp.where(hit(r, c), 1.0, 0.0).astype(BF)


def halves(x, axis):
    if axis == 0:
        return x[:HALF], x[HALF:]
    return x[:, :HALF], x[:, HALF:]


def butterfly(x, axis):
    first, second = halves(x, axis)
    return first + second, first - second


def join(a, b, axis):
    return jnp.concatenate([a, b], axis=axis)


def right_mul(x, tab, k):
    x = x.astype(BF)
    return dot(x, tab[k, 0]) + dot(x, tab[k, 1])


def left_mul(x, tab, k):
    x = x.astype(BF)
    return dot(tab[k, 0], x) + dot(tab[k, 1], x)


def columns_in(re, im, tab, k):
    sr, dr = butterfly(re, 1)
    si, di = butterfly(im, 1)
    a = right_mul(join(sr, si, 1), tab, k)
    b = right_mul(join(dr, di, 1), tab, k + 1)
    ar, ai = halves(a, 1)
    br, bi = halves(b, 1)
    return join(ar, br, 1), join(ai, bi, 1)


def rows_in(re, im, tab, k):
    sr, dr = butterfly(re, 0)
    si, di = butterfly(im, 0)
    a = left_mul(join(sr, si, 0), tab, k)
    b = left_mul(join(dr, di, 0), tab, k + 1)
    ar, ai = halves(a, 0)
    br, bi = halves(b, 0)
    return join(ar, br, 0), join(ai, bi, 0)


def rows_out(re, im, tab, k):
    re0, re1 = halves(re, 0)
    im0, im1 = halves(im, 0)
    a = left_mul(join(re0, im0, 0), tab, k)
    b = left_mul(join(re1, im1, 0), tab, k + 1)
    ar, ai = halves(a, 0)
    br, bi = halves(b, 0)
    return join(ar + br, ar - br, 0), join(ai + bi, ai - bi, 0)


def columns_out(re, im, tab, k):
    re0, re1 = halves(re, 1)
    im0, im1 = halves(im, 1)
    a = right_mul(join(re0, im0, 1), tab, k)
    b = right_mul(join(re1, im1, 1), tab, k + 1)
    ar, ai = halves(a, 1)
    br, bi = halves(b, 1)
    return join(ar + br, ar - br, 1), join(ai + bi, ai - bi, 1)


def propagate(re, im, tab, right, left):
    re, im = columns_in(re, im, tab, right)
    re, im = rows_in(re, im, tab, left)
    re, im = join(*butterfly(re, 0), 0), join(*butterfly(im, 0), 0)
    return join(*butterfly(re, 1), 1), join(*butterfly(im, 1), 1)


def keep(hit, x):
    return jnp.where(hit, x, jnp.zeros_like(x))


def rotated_columns(x, off):
    first, middle, last = x[:, :HALF], x[:, HALF:N], x[:, N:]
    lane = lax.broadcasted_iota(jnp.int32, first.shape, 1)
    return join(jnp.where(lane < off, last, first), middle, 1)


def object_columns(x, off):
    first = x[:, :HALF]
    lane = lax.broadcasted_iota(jnp.int32, first.shape, 1)
    return jnp.concatenate([keep(lane >= off, first), x[:, HALF:], keep(lane < off, first)], axis=1)


def rows_below(shape, off):
    return lax.broadcasted_iota(jnp.int32, shape, 0) < off


def behind(x, off):
    return lax.rem(x - off + N, N)


def remote(src, dst, send, recv, axis, index):
    return pltpu.make_async_remote_copy(
        src_ref=src,
        dst_ref=dst,
        send_sem=send,
        recv_sem=recv,
        device_id={axis: index},
        device_id_type=MESH,
    )


def kernel(
    off_hbm, obj_hbm, probe_hbm, int_hbm, tab_hbm,
    out_ref, probe_out,
    off_ref, obj, tile, halo, patch, held, waves, current, gout, gin, detour, returned, rim, rim_in, tab, meas,
    blocks, gathered, turned, turned_in, pair, pair_in,
    load_sem, halo_send, halo_recv, patch_send, patch_recv, grad_send, grad_recv, detour_send, detour_recv, returned_send, returned_recv,
    rim_send, rim_recv, block_send, block_recv, turned_send, turned_recv, pair_send, pair_recv,
):
    d = lax.axis_index("depth")
    m = lax.axis_index("scan")
    above, below = lax.rem(m + 31, 32), lax.rem(m + 1, 32)
    core = lax.rem(m, 2)
    place = m // 2
    mate = m + 1 - 2 * core
    side, z = d // 8, lax.rem(d, 8)
    bench = [lax.rem(BENCH[0] * core + BENCH[1] * j + BENCH[2], 8) for j in range(2)]
    worker = [j * 8 + bench[j] for j in range(2)]

    def steps_in(place_z, j, steps):
        hit = jnp.bool_(False)
        for step in steps:
            hit = jnp.logical_or(hit, place_z == lax.rem(bench[j] + step, 8))
        return hit

    detoured = [jnp.logical_and(side != j, steps_in(z, j, IN_STEPS[j])) for j in range(2)]
    mine = [d == w for w in worker]
    working = jnp.logical_or(mine[0], mine[1])

    def either(a, b):
        return jnp.logical_or(a, b)

    carries = [jnp.logical_and(side == j, steps_in(z, j, IN_STEPS[j])) for j in range(2)]
    hub = [d == (1 - j) * 8 + bench[j] for j in range(2)]
    handed = [jnp.logical_and(side != j, steps_in(z, j, OUT_STEPS[j])) for j in range(2)]

    def one(hit):
        return jnp.where(hit, 1, 0)

    greetings = jnp.where(working, 18, 4) + one(either(*detoured)) + sum(len(OUT_STEPS[j]) * one(hub[j]) for j in range(2))
    off_copy = pltpu.make_async_copy(off_hbm, off_ref, load_sem.at[0])
    obj_copy = pltpu.make_async_copy(obj_hbm.at[0], obj, load_sem.at[1])
    tab_copy = pltpu.make_async_copy(tab_hbm, tab, load_sem.at[2])
    meas_copy = [pltpu.make_async_copy(int_hbm.at[j], meas, load_sem.at[3]) for j in range(2)]
    probe_copy = pltpu.make_async_copy(probe_hbm, current, load_sem.at[4])
    obj_copy.start()
    off_copy.start()

    for j in range(2):

        @pl.when(mine[j])
        def _():
            probe_copy.start()
            meas_copy[j].start()
            tab_copy.start()

    barrier = pltpu.get_barrier_semaphore()

    @pl.when(working)
    def _():
        def greet(k, c):
            @pl.when(k != d)
            def _():
                pl.semaphore_signal(barrier, inc=1, device_id={"depth": k}, device_id_type=MESH)

            return c

        lax.fori_loop(0, SLICES, greet, 0)

    for t in (above, below):
        pl.semaphore_signal(barrier, inc=1, device_id={"scan": t}, device_id_type=MESH)
    @pl.when(either(*carries))
    def _():
        pl.semaphore_signal(barrier, inc=1, device_id={"depth": lax.rem(d + 8, 16)}, device_id_type=MESH)

    for j in range(2):

        @pl.when(handed[j])
        def _():
            centre = (1 - j) * 8 + bench[j]
            pl.semaphore_signal(barrier, inc=1, device_id={"depth": centre}, device_id_type=MESH)

    def greet_place(k, c):
        @pl.when(k != place)
        def _():
            pl.semaphore_signal(barrier, inc=1, device_id={"scan": 2 * k + core}, device_id_type=MESH)

        return c

    @pl.when(working)
    def _():
        lax.fori_loop(0, 16, greet_place, 0)

    obj_copy.wait()
    tile[...] = obj[...].astype(BF)
    off_copy.wait()
    row_off = [off_ref[j, 0] for j in range(2)]
    col_off = [off_ref[j, 1] for j in range(2)]

    pl.semaphore_wait(barrier, greetings)

    down = remote(tile, halo.at[0], halo_send.at[0], halo_recv.at[0], "scan", below)
    up = remote(tile, halo.at[1], halo_send.at[1], halo_recv.at[1], "scan", above)
    down.start()
    up.start()

    def patch_copy(j, h):
        return remote(
            patch.at[j, h], held.at[d, h], patch_send.at[j, h], patch_recv.at[h, d], "depth", worker[j]
        )

    def patch_keep(j, h):
        return pltpu.make_async_copy(patch.at[j, h], held.at[d, h], patch_recv.at[h, d])

    def detour_in(j, h, to):
        return remote(patch.at[j, h], detour.at[h], patch_send.at[j, h], detour_recv.at[h], "depth", to)

    def detour_out(j, h):
        source = d + 8 - 16 * j
        return remote(
            detour.at[h], held.at[source, h], detour_send.at[h], patch_recv.at[h, source], "depth", worker[j]
        )

    def hand_in(h):
        for j in range(2):

            @pl.when(mine[j])
            def _():
                patch_keep(j, h).start()

            @pl.when(jnp.logical_not(jnp.logical_or(mine[j], detoured[j])))
            def _():
                patch_copy(j, h).start()

            @pl.when(detoured[j])
            def _():
                detour_in(j, h, d - 8 + 16 * j).start()

    for j in range(2):
        for c in range(2):
            patch[j, 1, c] = rotated_columns(obj[c], col_off[j]).astype(BF)
    hand_in(1)
    down.wait_recv()
    up.wait_recv()
    for c in range(2):
        over, under = halo[0, c].astype(F32), halo[1, c].astype(F32)
        for j in range(2):
            rows = jnp.where(rows_below(over.shape, row_off[j]), under, over)
            patch[j, 0, c] = rotated_columns(rows, col_off[j]).astype(BF)
    hand_in(0)

    def block_copy(k):
        return remote(
            blocks.at[k], gathered.at[place], block_send.at[k], block_recv.at[place], "scan", 2 * k + core
        )

    def block_wait(k):
        return remote(
            blocks.at[k], gathered.at[k], block_send.at[k], block_recv.at[k], "scan", 2 * k + core
        )

    def turned_copy(j, k):
        rows = pl.ds(pl.multiple_of(k * 16, 16), 16)
        return remote(turned.at[rows], turned_in.at[j], turned_send.at[k], turned_recv.at[j], "depth", k)

    def turned_keep(j):
        rows = pl.ds(pl.multiple_of(d * 16, 16), 16)
        return pltpu.make_async_copy(turned.at[rows], turned_in.at[j], turned_recv.at[j])

    for j in range(2):

        @pl.when(carries[j])
        def _():
            for h in (1, 0):
                detour_in(j, h, d).wait_recv()
                detour_out(j, h).start()

    def return_in(j, s):
        i = lax.rem(s, 8)
        return remote(
            gout.at[s], returned.at[i], grad_send.at[s], returned_recv.at[i], "depth", (1 - j) * 8 + bench[j]
        )

    def return_out(j, i):
        return remote(
            returned.at[i], gin.at[j], returned_send.at[i], grad_recv.at[j], "depth", (1 - j) * 8 + i
        )

    def work(j):
        probe_copy.wait()
        meas_copy[j].wait()
        tab_copy.wait()
        even_odd = one_hot((N, N), lambda r, c: c == jnp.where(r < HALF, 2 * r, 2 * r - (N - 1)))
        even_odd_t = one_hot((N, N), lambda r, c: r == jnp.where(c < HALF, 2 * c, 2 * c - (N - 1)))
        measured = meas[...]
        high = measured.astype(BF)
        low = (measured - high.astype(F32)).astype(BF)
        meas[...] = dot(dot(even_odd, high).astype(BF), even_odd_t) + dot(
            dot(even_odd, low).astype(BF), even_odd_t
        )
        turn_rows = one_hot((N, N), lambda r, c: c == behind(r, row_off[j]))
        turn_cols = one_hot((N, N), lambda r, c: r == behind(c, col_off[j]))
        for c in range(2):
            current[c] = dot(dot(turn_rows, current[c].astype(BF)).astype(BF), turn_cols)

        def wait_patch(s):
            for h in range(2):

                @pl.when(s == d)
                def _():
                    patch_keep(j, h).wait()

                @pl.when(s != d)
                def _():
                    remote(
                        patch.at[j, h], held.at[s, h], patch_send.at[j, h], patch_recv.at[h, s], "depth", worker[j]
                    ).wait_recv()

        def held_patch(s):
            return [join(held[s, 0, c], held[s, 1, c], 0).astype(F32) for c in range(2)]

        def exit_wave(s):
            wait_patch(s)
            wr, wi = current[0], current[1]
            waves[s, 0] = wr.astype(BF)
            waves[s, 1] = wi.astype(BF)
            pr, pi = held_patch(s)
            return wr * pr - wi * pi, wr * pi + wi * pr

        def forward(s, carry):
            re, im = exit_wave(s)
            re, im = propagate(re, im, tab, 0, 4)
            current[0] = re
            current[1] = im
            return carry

        lax.fori_loop(0, SLICES - 1, forward, 0)
        re, im = exit_wave(SLICES - 1)
        re, im = columns_in(re, im, tab, 2)
        re, im = rows_in(re, im, tab, 6)
        misfit = re * re + im * im - meas[...]
        re, im = rows_out(misfit * re, misfit * im, tab, 2)
        re, im = columns_out(re, im, tab, 6)
        current[0] = re
        current[1] = im

        def grad_copy(s):
            return remote(gout.at[s], gin.at[j], grad_send.at[s], grad_recv.at[j], "depth", s)

        def grad_keep(s):
            return pltpu.make_async_copy(gout.at[s], gin.at[j], grad_recv.at[j])

        def across(s):
            return jnp.logical_and(s // 8 != j, steps_in(lax.rem(s, 8), j, OUT_STEPS[j]))

        def send_grad(s):
            @pl.when(s == d)
            def _():
                grad_keep(s).start()

            @pl.when(across(s))
            def _():
                return_in(j, s).start()

            @pl.when(jnp.logical_and(s != d, jnp.logical_not(across(s))))
            def _():
                grad_copy(s).start()

        def through(s):
            gr, gi = current[0], current[1]
            wr, wi = waves[s, 0].astype(F32), waves[s, 1].astype(F32)
            for c, product in enumerate((wr * gr + wi * gi, wr * gi - wi * gr)):
                for h, rows in enumerate(halves(product.astype(BF), 0)):
                    gout[s, h, c] = rows

            @pl.when(jnp.logical_or(s < LATE[0], s >= LATE[1]))
            def _():
                send_grad(s)

            pr, pi = held_patch(s)
            return pr * gr + pi * gi, pr * gi - pi * gr

        def backward(i, carry):
            re, im = through(SLICES - 1 - i)
            re, im = propagate(re, im, tab, 4, 0)
            current[0] = re
            current[1] = im
            return carry

        lax.fori_loop(0, SLICES - 1, backward, 0)
        re, im = through(0)
        back_rows = one_hot((N, N), lambda r, c: r == behind(c, row_off[j]))
        back_cols = one_hot((N, N), lambda r, c: c == behind(r, col_off[j]))
        for c, part in enumerate((re, im)):
            straight = dot(dot(back_rows, part.astype(BF)).astype(BF), back_cols).astype(BF)
            for k in range(16):
                blocks[k, c] = straight[16 * k : 16 * k + 16]

        def send_block(k, carry):
            @pl.when(k != place)
            def _():
                block_copy(k).start()

            return carry

        lax.fori_loop(0, 16, send_block, 0)
        gathered[place] = blocks[place]

        def take_block(k, carry):
            @pl.when(k != place)
            def _():
                block_wait(k).wait_recv()

            return carry

        lax.fori_loop(0, 16, take_block, 0)
        total = gathered[0].astype(F32)
        for k in range(1, 16):
            total = total + gathered[k].astype(F32)
        tall = jnp.concatenate([total[0], total[1], jnp.zeros((HALF - 32, N), F32)], axis=0)
        turned[...] = jnp.transpose(tall).astype(BF)
        turned_keep(j).start()

        def turn(k, carry):
            @pl.when(k != d)
            def _():
                turned_copy(j, k).start()

            return carry

        lax.fori_loop(0, SLICES, turn, 0)

        def send_late(i, carry):
            send_grad(LATE[1] - 1 - i)
            return carry

        lax.fori_loop(0, LATE[1] - LATE[0], send_late, 0)

    for j in range(2):

        @pl.when(mine[j])
        def _():
            work(j)

        @pl.when(hub[j])
        def _():
            def pass_on(k, carry):
                i = 7 - k if j == 0 else lax.rem(LATE[0] + 7 - k, 8)

                @pl.when(steps_in(i, j, OUT_STEPS[j]))
                def _():
                    return_in(j, (1 - j) * 8 + i).wait_recv()
                    return_out(j, i).start()

                return carry

            lax.fori_loop(0, 8, pass_on, 0)

    for j in range(2):

        @pl.when(jnp.logical_not(mine[j]))
        def _():
            remote(gout.at[0], gin.at[j], grad_send.at[0], grad_recv.at[j], "depth", d).wait_recv()

        @pl.when(mine[j])
        def _():
            pltpu.make_async_copy(gout.at[d], gin.at[j], grad_recv.at[j]).wait()

    for c in range(2):
        own, over, under = 0.0, 0.0, 0.0
        for j in range(2):
            own = own + object_columns(gin[j, 1, c].astype(F32), col_off[j])
            edge = object_columns(gin[j, 0, c].astype(F32), col_off[j])
            low = rows_below(edge.shape, row_off[j])
            over = over + keep(jnp.logical_not(low), edge)
            under = under + keep(low, edge)
        out_ref[0, c] = own
        rim[0, c] = over.astype(BF)
        rim[1, c] = under.astype(BF)
    to_above = remote(rim.at[0], rim_in.at[0], rim_send.at[0], rim_recv.at[0], "scan", above)
    to_below = remote(rim.at[1], rim_in.at[1], rim_send.at[1], rim_recv.at[1], "scan", below)
    to_above.start()
    to_below.start()

    for j in range(2):

        @pl.when(mine[j])
        def _():
            turned_keep(j).wait()

        @pl.when(jnp.logical_not(mine[j]))
        def _():
            turned_copy(j, d).wait_recv()

    both = turned_in[0].astype(F32) + turned_in[1].astype(F32)
    pair[...] = both.astype(BF)
    to_mate = remote(pair, pair_in, pair_send, pair_recv, "scan", mate)
    to_mate.start()
    to_above.wait_recv()
    to_below.wait_recv()
    out_ref[0] = out_ref[0] + rim_in[0].astype(F32) + rim_in[1].astype(F32)

    to_mate.wait_recv()
    everything = both + pair_in[...].astype(F32)
    own = one_hot((16, HALF), lambda r, l: l == (r // 8) * 16 + core * 8 + lax.rem(r, 8))
    top = everything.astype(BF)
    rest = (everything - top.astype(F32)).astype(BF)
    lanes = (((1,), (1,)), ((), ()))
    final = lax.dot_general(own, top, lanes, preferred_element_type=F32) + lax.dot_general(
        own, rest, lanes, preferred_element_type=F32
    )
    probe_out[0] = final[:8]
    probe_out[1] = final[8:]

    down.wait_send()
    up.wait_send()
    to_above.wait_send()
    to_below.wait_send()
    to_mate.wait_send()

    for j in range(2):

        @pl.when(jnp.logical_not(mine[j]))
        def _():
            patch_copy(j, 0).wait_send()
            patch_copy(j, 1).wait_send()

        @pl.when(carries[j])
        def _():
            for h in range(2):
                detour_out(j, h).wait_send()

        @pl.when(hub[j])
        def _():
            def passed(i, carry):
                @pl.when(steps_in(i, j, OUT_STEPS[j]))
                def _():
                    return_out(j, i).wait_send()

                return carry

            lax.fori_loop(0, 8, passed, 0)

        @pl.when(mine[j])
        def _():
            def sent(s, carry):
                @pl.when(s != d)
                def _():
                    remote(gout.at[s], gin.at[j], grad_send.at[s], grad_recv.at[j], "depth", s).wait_send()
                    turned_copy(j, s).wait_send()

                @pl.when(s != place)
                def _():
                    block_copy(s).wait_send()

                return carry

            lax.fori_loop(0, SLICES, sent, 0)


def results(grad_ref, probe_ref, out_ref, probe_out):
    out_ref[...] = grad_ref[...]
    probe_out[...] = probe_ref[...]


def per_device(tab, object_slices, probe, offsets, intensity):
    vmem = pl.BlockSpec(memory_space=pltpu.VMEM)
    anywhere = pl.BlockSpec(memory_space=pl.ANY)
    plane = (2, N, N)
    strip = (2, TILE, COLS)
    parts = (2, 2, HALF, N)
    dma = pltpu.SemaphoreType.DMA
    outs = (
        jax.ShapeDtypeStruct(object_slices.shape, F32),
        jax.ShapeDtypeStruct((2, 8, 16), F32),
    )
    grads = pl.pallas_call(
        kernel,
        out_shape=outs,
        in_specs=[anywhere] * 5,
        out_specs=(vmem, vmem),
        scratch_shapes=[
            pltpu.SMEM(offsets.shape, jnp.int32),
            pltpu.VMEM(strip, F32),
            pltpu.VMEM(strip, BF),
            pltpu.VMEM((2, *strip), BF),
            pltpu.VMEM((2, *parts), BF),
            pltpu.VMEM((SLICES, *parts), BF),
            pltpu.VMEM((SLICES, *plane), BF),
            pltpu.VMEM(plane, F32),
            pltpu.VMEM((SLICES, *parts), BF),
            pltpu.VMEM((2, *parts), BF),
            pltpu.VMEM(parts, BF),
            pltpu.VMEM((8, *parts), BF),
            pltpu.VMEM((2, *strip), BF),
            pltpu.VMEM((2, *strip), BF),
            pltpu.VMEM((8, 2, N, N), BF),
            pltpu.VMEM((N, N), F32),
            pltpu.VMEM((16, 2, 16, N), BF),
            pltpu.VMEM((16, 2, 16, N), BF),
            pltpu.VMEM((N, HALF), BF),
            pltpu.VMEM((2, 16, HALF), BF),
            pltpu.VMEM((16, HALF), BF),
            pltpu.VMEM((16, HALF), BF),
            dma((5,)),
            dma((2,)),
            dma((2,)),
            dma((2, 2)),
            dma((2, SLICES)),
            dma((SLICES,)),
            dma((2,)),
            dma((2,)),
            dma((2,)),
            dma((8,)),
            dma((8,)),
            dma((2,)),
            dma((2,)),
            dma((16,)),
            dma((16,)),
            dma((SLICES,)),
            dma((2,)),
            dma,
            dma,
        ],
        compiler_params=pltpu.CompilerParams(
            collective_id=0, has_side_effects=True, vmem_limit_bytes=60 << 20
        ),
        name="ptychography_chains",
    )(offsets, object_slices, probe, intensity, tab)
    return pl.pallas_call(
        results,
        out_shape=outs,
        in_specs=[vmem] * 2,
        out_specs=(vmem, vmem),
        name="results",
    )(*grads)


def solution(mesh):
    tab = tables()
    placed = (P("depth", None, "scan", None), P(), P("scan", None), P("scan", None, None))
    return jax.shard_map(
        lambda *args: per_device(jnp.asarray(tab), *args),
        mesh=mesh,
        in_specs=placed,
        out_specs=(P("depth", None, "scan", None), P(None, "scan", "depth")),
        check_vma=False,
    )
```

```python
import math

import jax
import jax.numpy as jnp
import ml_dtypes
import numpy as np
from jax import lax
from jax.experimental import pallas as pl
from jax.experimental.pallas import tpu as pltpu
from jax.sharding import PartitionSpec as P

MESH = pl.DeviceIdType.MESH
N = 256
HALF = 128
TILE = 128
COLS = 384
SLICES = 16
PHASE_SCALE = 16.0
BF = jnp.bfloat16
F32 = jnp.float32
IN_STEPS = ((), (1, 7))
OUT_STEPS = ((), ())
LATE = (5, 8)
BENCH = (4, 2, 0)


def real_form(table):
    return np.block([[table.real, table.imag], [-table.imag, table.real]])


def tables():
    n = np.arange(N)
    dft = np.exp(-2j * math.pi * (np.outer(n, n) % N) / N) / math.sqrt(N)
    q = ((n + HALF) % N - HALF) / N
    circulant = dft.conj() @ np.diag(np.exp(-1j * PHASE_SCALE * math.pi * q * q)) @ dft
    upper, lower = circulant[:HALF, :HALF], circulant[HALF:, :HALF]
    right = [
        real_form((upper + lower) / 2),
        real_form((upper - lower) / 2),
        real_form(dft[:HALF, 0::2]),
        real_form(dft[:HALF, 1::2]),
    ]
    full = np.stack(right + [t.T for t in right]).astype(np.float32)
    high = full.astype(ml_dtypes.bfloat16)
    low = (full - high.astype(np.float32)).astype(ml_dtypes.bfloat16)
    return np.stack([high, low], axis=1)


def dot(a, b):
    return jnp.dot(a, b, preferred_element_type=F32)


def one_hot(shape, hit):
    r = lax.broadcasted_iota(jnp.int32, shape, 0)
    c = lax.broadcasted_iota(jnp.int32, shape, 1)
    return jnp.where(hit(r, c), 1.0, 0.0).astype(BF)


def halves(x, axis):
    if axis == 0:
        return x[:HALF], x[HALF:]
    return x[:, :HALF], x[:, HALF:]


def butterfly(x, axis):
    first, second = halves(x, axis)
    return first + second, first - second


def join(a, b, axis):
    return jnp.concatenate([a, b], axis=axis)


def right_mul(x, tab, k):
    x = x.astype(BF)
    return dot(x, tab[k, 0]) + dot(x, tab[k, 1])


def left_mul(x, tab, k):
    x = x.astype(BF)
    return dot(tab[k, 0], x) + dot(tab[k, 1], x)


def columns_in(re, im, tab, k):
    sr, dr = butterfly(re, 1)
    si, di = butterfly(im, 1)
    a = right_mul(join(sr, si, 1), tab, k)
    b = right_mul(join(dr, di, 1), tab, k + 1)
    ar, ai = halves(a, 1)
    br, bi = halves(b, 1)
    return join(ar, br, 1), join(ai, bi, 1)


def rows_in(re, im, tab, k):
    sr, dr = butterfly(re, 0)
    si, di = butterfly(im, 0)
    a = left_mul(join(sr, si, 0), tab, k)
    b = left_mul(join(dr, di, 0), tab, k + 1)
    ar, ai = halves(a, 0)
    br, bi = halves(b, 0)
    return join(ar, br, 0), join(ai, bi, 0)


def rows_out(re, im, tab, k):
    re0, re1 = halves(re, 0)
    im0, im1 = halves(im, 0)
    a = left_mul(join(re0, im0, 0), tab, k)
    b = left_mul(join(re1, im1, 0), tab, k + 1)
    ar, ai = halves(a, 0)
    br, bi = halves(b, 0)
    return join(ar + br, ar - br, 0), join(ai + bi, ai - bi, 0)


def columns_out(re, im, tab, k):
    re0, re1 = halves(re, 1)
    im0, im1 = halves(im, 1)
    a = right_mul(join(re0, im0, 1), tab, k)
    b = right_mul(join(re1, im1, 1), tab, k + 1)
    ar, ai = halves(a, 1)
    br, bi = halves(b, 1)
    return join(ar + br, ar - br, 1), join(ai + bi, ai - bi, 1)


def propagate(re, im, tab, right, left):
    re, im = columns_in(re, im, tab, right)
    re, im = rows_in(re, im, tab, left)
    re, im = join(*butterfly(re, 0), 0), join(*butterfly(im, 0), 0)
    return join(*butterfly(re, 1), 1), join(*butterfly(im, 1), 1)


def keep(hit, x):
    return jnp.where(hit, x, jnp.zeros_like(x))


def rotated_columns(x, off):
    first, middle, last = x[:, :HALF], x[:, HALF:N], x[:, N:]
    lane = lax.broadcasted_iota(jnp.int32, first.shape, 1)
    return join(jnp.where(lane < off, last, first), middle, 1)


def object_columns(x, off):
    first = x[:, :HALF]
    lane = lax.broadcasted_iota(jnp.int32, first.shape, 1)
    return jnp.concatenate([keep(lane >= off, first), x[:, HALF:], keep(lane < off, first)], axis=1)


def rows_below(shape, off):
    return lax.broadcasted_iota(jnp.int32, shape, 0) < off


def behind(x, off):
    return lax.rem(x - off + N, N)


def remote(src, dst, send, recv, axis, index):
    return pltpu.make_async_remote_copy(
        src_ref=src,
        dst_ref=dst,
        send_sem=send,
        recv_sem=recv,
        device_id={axis: index},
        device_id_type=MESH,
    )


def kernel(
    off_hbm, obj_hbm, probe_hbm, int_hbm, tab_hbm,
    out_ref, probe_out,
    off_ref, obj, tile, halo, patch, held, waves, current, gout, gin, detour, returned, rim, rim_in, tab, meas,
    blocks, gathered, turned, turned_in, pair, pair_in,
    load_sem, halo_send, halo_recv, patch_send, patch_recv, grad_send, grad_recv, detour_send, detour_recv, returned_send, returned_recv,
    rim_send, rim_recv, block_send, block_recv, turned_send, turned_recv, pair_send, pair_recv,
):
    d = lax.axis_index("depth")
    m = lax.axis_index("scan")
    above, below = lax.rem(m + 31, 32), lax.rem(m + 1, 32)
    core = lax.rem(m, 2)
    place = m // 2
    mate = m + 1 - 2 * core
    side, z = d // 8, lax.rem(d, 8)
    bench = [lax.rem(BENCH[0] * core + BENCH[1] * j + BENCH[2], 8) for j in range(2)]
    worker = [j * 8 + bench[j] for j in range(2)]

    def steps_in(place_z, j, steps):
        hit = jnp.bool_(False)
        for step in steps:
            hit = jnp.logical_or(hit, place_z == lax.rem(bench[j] + step, 8))
        return hit

    detoured = [jnp.logical_and(side != j, steps_in(z, j, IN_STEPS[j])) for j in range(2)]
    mine = [d == w for w in worker]
    working = jnp.logical_or(mine[0], mine[1])

    def either(a, b):
        return jnp.logical_or(a, b)

    carries = [jnp.logical_and(side == j, steps_in(z, j, IN_STEPS[j])) for j in range(2)]
    hub = [d == (1 - j) * 8 + bench[j] for j in range(2)]
    handed = [jnp.logical_and(side != j, steps_in(z, j, OUT_STEPS[j])) for j in range(2)]

    def one(hit):
        return jnp.where(hit, 1, 0)

    greetings = jnp.where(working, 18, 4) + one(either(*detoured)) + sum(len(OUT_STEPS[j]) * one(hub[j]) for j in range(2))
    off_copy = pltpu.make_async_copy(off_hbm, off_ref, load_sem.at[0])
    obj_copy = pltpu.make_async_copy(obj_hbm.at[0], obj, load_sem.at[1])
    tab_copy = pltpu.make_async_copy(tab_hbm, tab, load_sem.at[2])
    meas_copy = [pltpu.make_async_copy(int_hbm.at[j], meas, load_sem.at[3]) for j in range(2)]
    probe_copy = pltpu.make_async_copy(probe_hbm, current, load_sem.at[4])
    obj_copy.start()
    off_copy.start()

    for j in range(2):

        @pl.when(mine[j])
        def _():
            probe_copy.start()
            meas_copy[j].start()
            tab_copy.start()

    barrier = pltpu.get_barrier_semaphore()

    @pl.when(working)
    def _():
        def greet(k, c):
            @pl.when(k != d)
            def _():
                pl.semaphore_signal(barrier, inc=1, device_id={"depth": k}, device_id_type=MESH)

            return c

        lax.fori_loop(0, SLICES, greet, 0)

    for t in (above, below):
        pl.semaphore_signal(barrier, inc=1, device_id={"scan": t}, device_id_type=MESH)
    @pl.when(either(*carries))
    def _():
        pl.semaphore_signal(barrier, inc=1, device_id={"depth": lax.rem(d + 8, 16)}, device_id_type=MESH)

    for j in range(2):

        @pl.when(handed[j])
        def _():
            centre = (1 - j) * 8 + bench[j]
            pl.semaphore_signal(barrier, inc=1, device_id={"depth": centre}, device_id_type=MESH)

    def greet_place(k, c):
        @pl.when(k != place)
        def _():
            pl.semaphore_signal(barrier, inc=1, device_id={"scan": 2 * k + core}, device_id_type=MESH)

        return c

    @pl.when(working)
    def _():
        lax.fori_loop(0, 16, greet_place, 0)

    obj_copy.wait()
    tile[...] = obj[...].astype(BF)
    off_copy.wait()
    row_off = [off_ref[j, 0] for j in range(2)]
    col_off = [off_ref[j, 1] for j in range(2)]

    pl.semaphore_wait(barrier, greetings)

    down = remote(tile, halo.at[0], halo_send.at[0], halo_recv.at[0], "scan", below)
    up = remote(tile, halo.at[1], halo_send.at[1], halo_recv.at[1], "scan", above)
    down.start()
    up.start()

    def patch_copy(j, h):
        return remote(
            patch.at[j, h], held.at[d, h], patch_send.at[j, h], patch_recv.at[h, d], "depth", worker[j]
        )

    def patch_keep(j, h):
        return pltpu.make_async_copy(patch.at[j, h], held.at[d, h], patch_recv.at[h, d])

    def detour_in(j, h, to):
        return remote(patch.at[j, h], detour.at[h], patch_send.at[j, h], detour_recv.at[h], "depth", to)

    def detour_out(j, h):
        source = d + 8 - 16 * j
        return remote(
            detour.at[h], held.at[source, h], detour_send.at[h], patch_recv.at[h, source], "depth", worker[j]
        )

    def hand_in(h):
        for j in range(2):

            @pl.when(mine[j])
            def _():
                patch_keep(j, h).start()

            @pl.when(jnp.logical_not(jnp.logical_or(mine[j], detoured[j])))
            def _():
                patch_copy(j, h).start()

            @pl.when(detoured[j])
            def _():
                detour_in(j, h, d - 8 + 16 * j).start()

    for j in range(2):
        for c in range(2):
            patch[j, 1, c] = rotated_columns(obj[c], col_off[j]).astype(BF)
    hand_in(1)
    down.wait_recv()
    up.wait_recv()
    for c in range(2):
        over, under = halo[0, c].astype(F32), halo[1, c].astype(F32)
        for j in range(2):
            rows = jnp.where(rows_below(over.shape, row_off[j]), under, over)
            patch[j, 0, c] = rotated_columns(rows, col_off[j]).astype(BF)
    hand_in(0)

    def block_copy(k):
        return remote(
            blocks.at[k], gathered.at[place], block_send.at[k], block_recv.at[place], "scan", 2 * k + core
        )

    def block_wait(k):
        return remote(
            blocks.at[k], gathered.at[k], block_send.at[k], block_recv.at[k], "scan", 2 * k + core
        )

    def turned_copy(j, k):
        rows = pl.ds(pl.multiple_of(k * 16, 16), 16)
        return remote(turned.at[rows], turned_in.at[j], turned_send.at[k], turned_recv.at[j], "depth", k)

    def turned_keep(j):
        rows = pl.ds(pl.multiple_of(d * 16, 16), 16)
        return pltpu.make_async_copy(turned.at[rows], turned_in.at[j], turned_recv.at[j])

    for j in range(2):

        @pl.when(carries[j])
        def _():
            for h in (1, 0):
                detour_in(j, h, d).wait_recv()
                detour_out(j, h).start()

    def return_in(j, s):
        i = lax.rem(s, 8)
        return remote(
            gout.at[s], returned.at[i], grad_send.at[s], returned_recv.at[i], "depth", (1 - j) * 8 + bench[j]
        )

    def return_out(j, i):
        return remote(
            returned.at[i], gin.at[j], returned_send.at[i], grad_recv.at[j], "depth", (1 - j) * 8 + i
        )

    def work(j):
        probe_copy.wait()
        meas_copy[j].wait()
        tab_copy.wait()
        even_odd = one_hot((N, N), lambda r, c: c == jnp.where(r < HALF, 2 * r, 2 * r - (N - 1)))
        even_odd_t = one_hot((N, N), lambda r, c: r == jnp.where(c < HALF, 2 * c, 2 * c - (N - 1)))
        measured = meas[...]
        high = measured.astype(BF)
        low = (measured - high.astype(F32)).astype(BF)
        meas[...] = dot(dot(even_odd, high).astype(BF), even_odd_t) + dot(
            dot(even_odd, low).astype(BF), even_odd_t
        )
        turn_rows = one_hot((N, N), lambda r, c: c == behind(r, row_off[j]))
        turn_cols = one_hot((N, N), lambda r, c: r == behind(c, col_off[j]))
        for c in range(2):
            current[c] = dot(dot(turn_rows, current[c].astype(BF)).astype(BF), turn_cols)

        def wait_patch(s):
            for h in range(2):

                @pl.when(s == d)
                def _():
                    patch_keep(j, h).wait()

                @pl.when(s != d)
                def _():
                    remote(
                        patch.at[j, h], held.at[s, h], patch_send.at[j, h], patch_recv.at[h, s], "depth", worker[j]
                    ).wait_recv()

        def held_patch(s):
            return [join(held[s, 0, c], held[s, 1, c], 0).astype(F32) for c in range(2)]

        def exit_wave(s):
            wait_patch(s)
            wr, wi = current[0], current[1]
            waves[s, 0] = wr.astype(BF)
            waves[s, 1] = wi.astype(BF)
            pr, pi = held_patch(s)
            return wr * pr - wi * pi, wr * pi + wi * pr

        def forward(s, carry):
            re, im = exit_wave(s)
            re, im = propagate(re, im, tab, 0, 4)
            current[0] = re
            current[1] = im
            return carry

        lax.fori_loop(0, SLICES - 1, forward, 0)
        re, im = exit_wave(SLICES - 1)
        re, im = columns_in(re, im, tab, 2)
        re, im = rows_in(re, im, tab, 6)
        misfit = re * re + im * im - meas[...]
        re, im = rows_out(misfit * re, misfit * im, tab, 2)
        re, im = columns_out(re, im, tab, 6)
        current[0] = re
        current[1] = im

        def grad_copy(s):
            return remote(gout.at[s], gin.at[j], grad_send.at[s], grad_recv.at[j], "depth", s)

        def grad_keep(s):
            return pltpu.make_async_copy(gout.at[s], gin.at[j], grad_recv.at[j])

        def across(s):
            return jnp.logical_and(s // 8 != j, steps_in(lax.rem(s, 8), j, OUT_STEPS[j]))

        def send_grad(s):
            @pl.when(s == d)
            def _():
                grad_keep(s).start()

            @pl.when(across(s))
            def _():
                return_in(j, s).start()

            @pl.when(jnp.logical_and(s != d, jnp.logical_not(across(s))))
            def _():
                for h in range(2):
                    remote(
                        gout.at[s, h], gin.at[j, h], grad_send.at[s], grad_recv.at[j], "depth", s
                    ).start()

        def through(s):
            gr, gi = current[0], current[1]
            wr, wi = waves[s, 0].astype(F32), waves[s, 1].astype(F32)
            for c, product in enumerate((wr * gr + wi * gi, wr * gi - wi * gr)):
                for h, rows in enumerate(halves(product.astype(BF), 0)):
                    gout[s, h, c] = rows

            @pl.when(jnp.logical_or(s < LATE[0], s >= LATE[1]))
            def _():
                send_grad(s)

            pr, pi = held_patch(s)
            return pr * gr + pi * gi, pr * gi - pi * gr

        def backward(i, carry):
            re, im = through(SLICES - 1 - i)
            re, im = propagate(re, im, tab, 4, 0)
            current[0] = re
            current[1] = im
            return carry

        lax.fori_loop(0, SLICES - 1, backward, 0)
        re, im = through(0)
        back_rows = one_hot((N, N), lambda r, c: r == behind(c, row_off[j]))
        back_cols = one_hot((N, N), lambda r, c: c == behind(r, col_off[j]))
        for c, part in enumerate((re, im)):
            straight = dot(dot(back_rows, part.astype(BF)).astype(BF), back_cols).astype(BF)
            for k in range(16):
                blocks[k, c] = straight[16 * k : 16 * k + 16]

        def send_block(k, carry):
            @pl.when(k != place)
            def _():
                block_copy(k).start()

            return carry

        lax.fori_loop(0, 16, send_block, 0)
        gathered[place] = blocks[place]

        def take_block(k, carry):
            @pl.when(k != place)
            def _():
                block_wait(k).wait_recv()

            return carry

        lax.fori_loop(0, 16, take_block, 0)
        total = gathered[0].astype(F32)
        for k in range(1, 16):
            total = total + gathered[k].astype(F32)
        tall = jnp.concatenate([total[0], total[1], jnp.zeros((HALF - 32, N), F32)], axis=0)
        turned[...] = jnp.transpose(tall).astype(BF)
        turned_keep(j).start()

        def turn(k, carry):
            @pl.when(k != d)
            def _():
                turned_copy(j, k).start()

            return carry

        lax.fori_loop(0, SLICES, turn, 0)

        def send_late(i, carry):
            send_grad(LATE[0] + i)
            return carry

        lax.fori_loop(0, LATE[1] - LATE[0], send_late, 0)

    for j in range(2):

        @pl.when(mine[j])
        def _():
            work(j)

        @pl.when(hub[j])
        def _():
            def pass_on(k, carry):
                i = 7 - k if j == 0 else lax.rem(LATE[0] + 7 - k, 8)

                @pl.when(steps_in(i, j, OUT_STEPS[j]))
                def _():
                    return_in(j, (1 - j) * 8 + i).wait_recv()
                    return_out(j, i).start()

                return carry

            lax.fori_loop(0, 8, pass_on, 0)

    for j in range(2):

        @pl.when(jnp.logical_not(mine[j]))
        def _():
            remote(gout.at[0], gin.at[j], grad_send.at[0], grad_recv.at[j], "depth", d).wait_recv()

        @pl.when(mine[j])
        def _():
            pltpu.make_async_copy(gout.at[d], gin.at[j], grad_recv.at[j]).wait()

    for c in range(2):
        own, over, under = 0.0, 0.0, 0.0
        for j in range(2):
            own = own + object_columns(gin[j, 1, c].astype(F32), col_off[j])
            edge = object_columns(gin[j, 0, c].astype(F32), col_off[j])
            low = rows_below(edge.shape, row_off[j])
            over = over + keep(jnp.logical_not(low), edge)
            under = under + keep(low, edge)
        out_ref[0, c] = own
        rim[0, c] = over.astype(BF)
        rim[1, c] = under.astype(BF)
    to_above = remote(rim.at[0], rim_in.at[0], rim_send.at[0], rim_recv.at[0], "scan", above)
    to_below = remote(rim.at[1], rim_in.at[1], rim_send.at[1], rim_recv.at[1], "scan", below)
    to_above.start()
    to_below.start()

    for j in range(2):

        @pl.when(mine[j])
        def _():
            turned_keep(j).wait()

        @pl.when(jnp.logical_not(mine[j]))
        def _():
            turned_copy(j, d).wait_recv()

    both = turned_in[0].astype(F32) + turned_in[1].astype(F32)
    pair[...] = both.astype(BF)
    to_mate = remote(pair, pair_in, pair_send, pair_recv, "scan", mate)
    to_mate.start()
    to_above.wait_recv()
    to_below.wait_recv()
    out_ref[0] = out_ref[0] + rim_in[0].astype(F32) + rim_in[1].astype(F32)

    to_mate.wait_recv()
    everything = both + pair_in[...].astype(F32)
    own = one_hot((16, HALF), lambda r, l: l == (r // 8) * 16 + core * 8 + lax.rem(r, 8))
    top = everything.astype(BF)
    rest = (everything - top.astype(F32)).astype(BF)
    lanes = (((1,), (1,)), ((), ()))
    final = lax.dot_general(own, top, lanes, preferred_element_type=F32) + lax.dot_general(
        own, rest, lanes, preferred_element_type=F32
    )
    probe_out[0] = final[:8]
    probe_out[1] = final[8:]

    down.wait_send()
    up.wait_send()
    to_above.wait_send()
    to_below.wait_send()
    to_mate.wait_send()

    for j in range(2):

        @pl.when(jnp.logical_not(mine[j]))
        def _():
            patch_copy(j, 0).wait_send()
            patch_copy(j, 1).wait_send()

        @pl.when(carries[j])
        def _():
            for h in range(2):
                detour_out(j, h).wait_send()

        @pl.when(hub[j])
        def _():
            def passed(i, carry):
                @pl.when(steps_in(i, j, OUT_STEPS[j]))
                def _():
                    return_out(j, i).wait_send()

                return carry

            lax.fori_loop(0, 8, passed, 0)

        @pl.when(mine[j])
        def _():
            def sent(s, carry):
                @pl.when(s != d)
                def _():
                    remote(gout.at[s], gin.at[j], grad_send.at[s], grad_recv.at[j], "depth", s).wait_send()
                    turned_copy(j, s).wait_send()

                @pl.when(s != place)
                def _():
                    block_copy(s).wait_send()

                return carry

            lax.fori_loop(0, SLICES, sent, 0)


def results(grad_ref, probe_ref, out_ref, probe_out):
    out_ref[...] = grad_ref[...]
    probe_out[...] = probe_ref[...]


def per_device(tab, object_slices, probe, offsets, intensity):
    vmem = pl.BlockSpec(memory_space=pltpu.VMEM)
    anywhere = pl.BlockSpec(memory_space=pl.ANY)
    plane = (2, N, N)
    strip = (2, TILE, COLS)
    parts = (2, 2, HALF, N)
    dma = pltpu.SemaphoreType.DMA
    outs = (
        jax.ShapeDtypeStruct(object_slices.shape, F32),
        jax.ShapeDtypeStruct((2, 8, 16), F32),
    )
    grads = pl.pallas_call(
        kernel,
        out_shape=outs,
        in_specs=[anywhere] * 5,
        out_specs=(vmem, vmem),
        scratch_shapes=[
            pltpu.SMEM(offsets.shape, jnp.int32),
            pltpu.VMEM(strip, F32),
            pltpu.VMEM(strip, BF),
            pltpu.VMEM((2, *strip), BF),
            pltpu.VMEM((2, *parts), BF),
            pltpu.VMEM((SLICES, *parts), BF),
            pltpu.VMEM((SLICES, *plane), BF),
            pltpu.VMEM(plane, F32),
            pltpu.VMEM((SLICES, *parts), BF),
            pltpu.VMEM((2, *parts), BF),
            pltpu.VMEM(parts, BF),
            pltpu.VMEM((8, *parts), BF),
            pltpu.VMEM((2, *strip), BF),
            pltpu.VMEM((2, *strip), BF),
            pltpu.VMEM((8, 2, N, N), BF),
            pltpu.VMEM((N, N), F32),
            pltpu.VMEM((16, 2, 16, N), BF),
            pltpu.VMEM((16, 2, 16, N), BF),
            pltpu.VMEM((N, HALF), BF),
            pltpu.VMEM((2, 16, HALF), BF),
            pltpu.VMEM((16, HALF), BF),
            pltpu.VMEM((16, HALF), BF),
            dma((5,)),
            dma((2,)),
            dma((2,)),
            dma((2, 2)),
            dma((2, SLICES)),
            dma((SLICES,)),
            dma((2,)),
            dma((2,)),
            dma((2,)),
            dma((8,)),
            dma((8,)),
            dma((2,)),
            dma((2,)),
            dma((16,)),
            dma((16,)),
            dma((SLICES,)),
            dma((2,)),
            dma,
            dma,
        ],
        compiler_params=pltpu.CompilerParams(
            collective_id=0, has_side_effects=True, vmem_limit_bytes=60 << 20
        ),
        name="ptychography_chains",
    )(offsets, object_slices, probe, intensity, tab)
    return pl.pallas_call(
        results,
        out_shape=outs,
        in_specs=[vmem] * 2,
        out_specs=(vmem, vmem),
        name="results",
    )(*grads)


def solution(mesh):
    tab = tables()
    placed = (P("depth", None, "scan", None), P(), P("scan", None), P("scan", None, None))
    return jax.shard_map(
        lambda *args: per_device(jnp.asarray(tab), *args),
        mesh=mesh,
        in_specs=placed,
        out_specs=(P("depth", None, "scan", None), P(None, "scan", "depth")),
        check_vma=False,
    )
```
